32 devices in a mesh: dp: 8 (over z, y), shard: 4 (over x, core).
Axes of the slice: x: 2, y: 2, z: 4, core: 2. Of those that a mesh axis runs over, the one named last changes fastest.
Arguments:
- key_grad: bfloat16 [8, 512, 2560], P('dp', 'shard'), may hold values from -90 to 90
- key_error: float32 [8, 512, 2560], P('dp', 'shard'), may hold values from -4 to 4
- router_grad: bfloat16 [8, 64, 2560], P('dp', 'shard'), may hold values from -90 to 90
- router_error: float32 [8, 64, 2560], P('dp', 'shard'), may hold values from -4 to 4
- norm_grad: bfloat16 [8, 2, 2560], P('dp', None, 'shard'), may hold values from -8 to 8
- key_basis: float32 [32, 2560], replicated, may hold values from -6 to 6
- router_basis: float32 [32, 2560], replicated, may hold values from -6 to 6
- key_momentum: float32 [512, 2560], P('shard', 'dp'), may hold values from -4 to 4
- key_weight: float32 [512, 2560], P('shard', 'dp'), may hold values from -4 to 4
- router_momentum: float32 [64, 2560], P('shard', 'dp'), may hold values from -4 to 4
- router_weight: float32 [64, 2560], P('shard', 'dp'), may hold values from -4 to 4
- norm_momentum: float32 [2, 2560], P(None, 'shard'), may hold values from -4 to 4
- norm_weight: float32 [2, 2560], P(None, 'shard'), may hold values from 0.5 to 1.5
Outputs:
- key_carry: float32 [8, 512, 2560], P('dp', 'shard')
- router_carry: float32 [8, 64, 2560], P('dp', 'shard')
- key_velocity: float32 [512, 2560], P('shard', 'dp')
- key_master: float32 [512, 2560], P('shard', 'dp')
- key_params: bfloat16 [512, 2560], P(None, 'dp')
- router_velocity: float32 [64, 2560], P('shard', 'dp')
- router_master: float32 [64, 2560], P('shard', 'dp')
- router_params: bfloat16 [64, 2560], P(None, 'dp')
- norm_velocity: float32 [2, 2560], P(None, 'shard')
- norm_master: float32 [2, 2560], P(None, 'shard')
- norm_params: bfloat16 [2, 2560], replicated
The draws below stay inside these ranges and needn't reach their ends.
All inputs are finite; a program needn't handle non-finite values.
Results may differ from the reference program's by a relative error of at most 0.008.
Values may be sent and summed in bfloat16 or wider, within the bound.
A program may use at most 64 MiB of HBM per device.

```python
import jax
import jax.numpy as jnp
from jax import lax

WIDTH = 2560
KEY_ROWS = 512
EXPERTS = 64
NORM_VECS = 2
FACTOR_RANK = 32
ROOT_STEPS = 4
REPLICAS = 8
N_DP = 8


def gradient_draw(key, replicas, row_count, col_count):
    noise_key, common_key, row_key, col_key, replica_key = jax.random.split(key, 5)
    noise_part = jnp.clip(jax.random.normal(noise_key, (replicas, row_count, col_count), jnp.float32), -5.0, 5.0)
    common = jnp.clip(jax.random.normal(common_key, (1, row_count, col_count), jnp.float32), -5.0, 5.0)
    replica_scale = 10.0 ** jax.random.uniform(replica_key, (replicas, 1, 1), jnp.float32, 0.0, 1.0)
    mixed = 0.2 * common + replica_scale * noise_part
    jitter = jax.random.uniform(row_key, (row_count,), jnp.float32, -0.15, 0.15)
    row_scale = 10.0 ** (jnp.arange(row_count, dtype=jnp.float32) / row_count + jitter)
    col_scale = 10.0 ** jax.random.uniform(col_key, (col_count,), jnp.float32, 0.0, 1.0)
    return 0.012 * mixed * row_scale[None, :, None] * col_scale[None, None, :]


def draw_key_grad(key, part):
    return gradient_draw(key, REPLICAS, KEY_ROWS, WIDTH).astype(jnp.bfloat16)


def draw_router_grad(key, part):
    return gradient_draw(key, REPLICAS, EXPERTS, WIDTH).astype(jnp.bfloat16)


def steps_of(rng, dims, pieces, smallest, top_value):
    loudness = 1.0
    for position, shards_of in pieces:
        draws = jax.random.uniform(jax.random.fold_in(jax.random.fold_in(rng, 6), position), (shards_of,), jnp.float32, smallest / len(pieces), top_value / len(pieces))
        loudness = loudness * jnp.repeat(jnp.exp(draws), dims[position] // shards_of).reshape((-1,) + (1,) * (len(dims) - 1 - position))
    return loudness


def normal_values(own_key, shape, deviation, most, cuts=(), held_as=jnp.bfloat16):
    result = jax.random.normal(own_key, shape, jnp.float32) * deviation
    if len(cuts) > 0:
        result = steps_of(own_key, shape, cuts, -0.22, 0.18) * result
    return jnp.clip(result, min=-most, max=most).astype(held_as)


def setup_inputs(seed: int = 0) -> dict:
    streams_of = jax.random.split(jax.random.key(seed), 14)
    return {
        "key_grad": draw_key_grad(jax.random.fold_in(streams_of[13], 71), 0),
        "key_error": normal_values(streams_of[1], (REPLICAS, KEY_ROWS, WIDTH), 0.3, 4.0, ((0, 8), (1, 4)), jnp.float32),
        "router_grad": draw_router_grad(jax.random.fold_in(streams_of[13], 71), 0),
        "router_error": normal_values(streams_of[3], (REPLICAS, EXPERTS, WIDTH), 0.3, 4.0, ((0, 8), (1, 4)), jnp.float32),
        "norm_grad": normal_values(streams_of[4], (REPLICAS, NORM_VECS, WIDTH), 2.0, 8.0, ((0, 8), (2, 4))),
        "key_basis": normal_values(streams_of[5], (FACTOR_RANK, WIDTH), 1.0, 6.0, (), jnp.float32),
        "router_basis": normal_values(streams_of[6], (FACTOR_RANK, WIDTH), 1.0, 6.0, (), jnp.float32),
        "key_momentum": normal_values(streams_of[7], (KEY_ROWS, WIDTH), 0.3, 4.0, ((0, 4), (1, 8)), jnp.float32),
        "key_weight": normal_values(streams_of[8], (KEY_ROWS, WIDTH), 0.3, 4.0, ((0, 4), (1, 8)), jnp.float32),
        "router_momentum": normal_values(streams_of[9], (EXPERTS, WIDTH), 0.3, 4.0, ((0, 4), (1, 8)), jnp.float32),
        "router_weight": normal_values(streams_of[10], (EXPERTS, WIDTH), 0.3, 4.0, ((0, 4), (1, 8)), jnp.float32),
        "norm_momentum": normal_values(streams_of[11], (NORM_VECS, WIDTH), 0.3, 4.0, ((1, 4),), jnp.float32),
        "norm_weight": jnp.clip(1.0 + 0.1 * jax.random.normal(streams_of[12], (NORM_VECS, WIDTH), jnp.float32), 0.5, 1.5),
    }


highest = lax.Precision.HIGHEST
momentum_decay = 0.9
learning_rate = 0.1

def inverse_root(gram_matrix):
    scaling = jnp.sqrt(jnp.sum(gram_matrix * gram_matrix)) + 1e-06
    identity = jnp.eye(gram_matrix.shape[0], dtype=jnp.float32)
    square_side = gram_matrix / scaling
    root_side = identity
    for sweep_index in range(ROOT_STEPS):
        middle = 1.5 * identity - 0.5 * jnp.dot(root_side, square_side, precision=highest)
        square_side = jnp.dot(square_side, middle, precision=highest)
        root_side = jnp.dot(middle, root_side, precision=highest)
    return (root_side, scaling)

def compress(gradient, residue, old_basis):
    merged = gradient.astype(jnp.float32) + residue
    summed = lax.optimization_barrier(jnp.sum(merged, axis=0))
    factor_rows = lax.dot_general(old_basis, summed, (((1,), (1,)), ((), ())), precision=highest)
    gram_matrix = lax.dot_general(factor_rows, factor_rows, (((1,), (1,)), ((), ())), precision=highest)
    root_side, scaling = inverse_root(gram_matrix)
    orthonormal = jnp.dot(root_side, factor_rows, precision=highest) / jnp.sqrt(scaling)
    columns = lax.dot_general(summed, orthonormal, (((0,), (1,)), ((), ())), precision=highest) / N_DP
    approx = lax.dot_general(orthonormal, columns, (((0,), (1,)), ((), ())), precision=highest)
    return (merged - approx[None], approx)

def advance(momentum, weight, direction):
    velocity = momentum_decay * momentum + direction
    master = weight - learning_rate * velocity
    return (velocity, master, master.astype(jnp.bfloat16))

def reference(key_grad, key_error, router_grad, router_error, norm_grad, key_basis, router_basis, key_momentum, key_weight, router_momentum, router_weight, norm_momentum, norm_weight):
    key_carry, approx_key = compress(key_grad, key_error, key_basis)
    router_carry, approx_router = compress(router_grad, router_error, router_basis)
    norm_mean = lax.optimization_barrier(jnp.sum(norm_grad.astype(jnp.float32), axis=0)) / N_DP
    key_velocity, key_master, key_params = advance(key_momentum, key_weight, approx_key)
    router_velocity, router_master, router_params = advance(router_momentum, router_weight, approx_router)
    norm_velocity, norm_master, norm_params = advance(norm_momentum, norm_weight, norm_mean)
    return (key_carry, router_carry, key_velocity, key_master, key_params, router_velocity, router_master, router_params, norm_velocity, norm_master, norm_params)
```

```python
import functools

import jax
import jax.numpy as jnp
from jax import lax
from jax.experimental import pallas as pl
from jax.experimental.pallas import tpu as pltpu
from jax.sharding import PartitionSpec as P

ROOT_STEPS = 4
MESH = pl.DeviceIdType.MESH
LANES = 128

highest = lax.Precision.HIGHEST
momentum_decay = 0.9
learning_rate = 0.1
f32 = jnp.float32
bf16 = jnp.bfloat16


def inverse_root(gram_matrix):
    scaling = jnp.sqrt(jnp.sum(gram_matrix * gram_matrix)) + 1e-06
    identity = jnp.eye(gram_matrix.shape[0], dtype=jnp.float32)
    square_side = gram_matrix / scaling
    root_side = identity
    for sweep_index in range(ROOT_STEPS):
        middle = 1.5 * identity - 0.5 * jnp.dot(root_side, square_side, precision=highest)
        square_side = jnp.dot(square_side, middle, precision=highest)
        root_side = jnp.dot(middle, root_side, precision=highest)
    return (root_side, scaling)


def project(old_basis, merged):
    return lax.dot_general(old_basis, merged, (((1,), (1,)), ((), ())), precision=highest)


def gram_of(factor_rows):
    return lax.dot_general(factor_rows, factor_rows, (((1,), (1,)), ((), ())), precision=highest)


def normalize(gram_matrix, factor_rows):
    root_side, scaling = inverse_root(gram_matrix)
    return jnp.dot(root_side, factor_rows, precision=highest) / jnp.sqrt(scaling)


def advance(momentum, weight, direction):
    velocity = momentum_decay * momentum + direction
    return (velocity, weight - learning_rate * velocity)


def general_body(
    key_grad,
    key_error,
    router_grad,
    router_error,
    norm_grad,
    key_basis,
    router_basis,
    key_momentum,
    key_weight,
    router_momentum,
    router_weight,
    norm_momentum,
    norm_weight,
):
    replicas = lax.axis_size("dp")
    rank_size = key_basis.shape[0]
    merged_key = key_grad[0].astype(jnp.float32) + key_error[0]
    merged_router = router_grad[0].astype(jnp.float32) + router_error[0]
    rows_key, rows_router, norm_sum = lax.psum(
        (
            project(key_basis, merged_key),
            project(router_basis, merged_router),
            norm_grad[0].astype(jnp.float32),
        ),
        "dp",
    )
    gram_key, gram_router = lax.psum((gram_of(rows_key), gram_of(rows_router)), "shard")
    ortho_key = normalize(gram_key, rows_key)
    ortho_router = normalize(gram_router, rows_router)
    key_part = lax.dot_general(merged_key, ortho_key, (((0,), (1,)), ((), ())), precision=highest)
    router_part = lax.dot_general(
        merged_router, ortho_router, (((0,), (1,)), ((), ())), precision=highest
    )
    column_sum = lax.psum(jnp.concatenate([key_part, router_part], axis=1), ("dp", "shard"))
    columns = column_sum / replicas
    approx_key = lax.dot_general(
        ortho_key, columns[:, :rank_size], (((0,), (1,)), ((), ())), precision=highest
    )
    approx_router = lax.dot_general(
        ortho_router, columns[:, rank_size:], (((0,), (1,)), ((), ())), precision=highest
    )
    col_width = key_momentum.shape[1]
    offset = lax.axis_index("dp") * col_width
    key_velocity, key_master = advance(
        key_momentum, key_weight, lax.dynamic_slice_in_dim(approx_key, offset, col_width, 1)
    )
    router_velocity, router_master = advance(
        router_momentum,
        router_weight,
        lax.dynamic_slice_in_dim(approx_router, offset, col_width, 1),
    )
    norm_velocity, norm_master = advance(norm_momentum, norm_weight, norm_sum / replicas)
    key_params, router_params, norm_params = (
        lax.all_gather(key_master.astype(jnp.bfloat16), "shard", axis=0, tiled=True),
        lax.all_gather(router_master.astype(jnp.bfloat16), "shard", axis=0, tiled=True),
        lax.all_gather(norm_master.astype(jnp.bfloat16), "shard", axis=1, tiled=True),
    )
    key_carry = (merged_key - approx_key)[None]
    router_carry = (merged_router - approx_router)[None]
    return (
        key_carry,
        router_carry,
        key_velocity,
        key_master,
        key_params,
        router_velocity,
        router_master,
        router_params,
        norm_velocity,
        norm_master,
        norm_params,
    )


def halves(x):
    high = x.astype(bf16)
    return high, (x - high.astype(f32)).astype(bf16)


def fold(x, rows, cols):
    y = x[:rows] + x[rows:]
    return y[:, :cols] + y[:, cols:]


def window(d):
    return (5 * d // 2) * LANES


def packed(x):
    pieces = [x[:, LANES * j : LANES * (j + 1)] for j in range(x.shape[1] // LANES)]
    rows = 2 * len(pieces)
    return jnp.concatenate(pieces + [jnp.zeros((16 - rows, LANES), f32)], axis=0)


def exchange_kernel(
    n_dp, n_shard, rank,
    kg, ke, rg, re, ng, kb, rb, km, kw, rm, rw, nm, nw,
    ortho, cols, ufull, nsum, npar,
    mk, mr, p64, recv1, recv2, nsend, nrecv, csend, crecv, bsend, brecv, send, recv,
):
    d = lax.axis_index("dp")
    s = lax.axis_index("shard")
    total = n_dp * n_shard
    me = d * n_shard + s
    core = lax.rem(s, 2)
    x = s // 2
    mate = s + 1 - 2 * core
    half = total // 2
    q = x * n_dp + d
    key_rows, width = mk.shape[0] // 2, mk.shape[1]
    router_rows = mr.shape[0] // 2

    def peer_all(j):
        t = lax.rem(me + j, total)
        return (t // n_shard, lax.rem(t, n_shard))

    barrier = pltpu.get_barrier_semaphore()

    def greet(j, carry):
        pl.semaphore_signal(barrier, inc=1, device_id=peer_all(j), device_id_type=MESH)
        return carry

    lax.fori_loop(1, total, greet, 0)

    def put(src, dst, which, device):
        pltpu.make_async_remote_copy(
            src_ref=src, dst_ref=dst, send_sem=send.at[which], recv_sem=recv.at[which],
            device_id=device, device_id_type=MESH,
        ).start()

    def wait_recv(ref, which):
        pltpu.make_async_copy(ref, ref, recv.at[which]).wait()

    def wait_send(ref, which):
        pltpu.make_async_copy(ref, ref, send.at[which]).wait()

    high, low = halves(kg[0].astype(f32) + ke[0])
    mk[:key_rows] = high
    mk[key_rows:] = low
    high, low = halves(rg[0].astype(f32) + re[0])
    mr[:router_rows] = high
    mr[router_rows:] = low
    nt = (((1,), (1,)), ((), ()))
    kb2 = jnp.concatenate(halves(kb[...]), axis=0)
    pk = lax.dot_general(kb2, mk[...], nt, preferred_element_type=f32)
    p64[:rank] = fold(pk, rank, key_rows)
    rb2 = jnp.concatenate(halves(rb[...]), axis=0)
    pr = lax.dot_general(rb2, mr[...], nt, preferred_element_type=f32)
    p64[rank:] = jnp.concatenate(
        [fold(pr, rank, router_rows), jnp.zeros((rank, LANES - router_rows), f32)], axis=1
    )
    nsend[0] = packed(ng[0].astype(f32)).astype(bf16)

    pl.semaphore_wait(barrier, total - 1)

    def send_rows(j, carry):
        t = lax.rem(d + j, n_dp)
        put(p64.at[pl.ds(pl.multiple_of(t * 8, 8), 8)], recv1.at[d], 0, (t, s))
        return carry

    lax.fori_loop(1, n_dp, send_rows, 0)

    def send_norm(j, carry):
        t = lax.rem(d + j, n_dp)
        put(nsend.at[0], nrecv.at[d], 1, (t, s))
        return carry

    lax.fori_loop(1, n_dp, send_norm, 0)
    recv1[d] = p64[pl.ds(pl.multiple_of(d * 8, 8), 8), :]
    nrecv[d] = nsend[0]
    wait_recv(recv1.at[pl.ds(0, n_dp - 1)], 0)
    slot = s * n_dp + d
    recv2[slot] = jnp.sum(recv1[...], axis=0)

    def send_sum(j, carry):
        put(recv2.at[slot], recv2.at[slot], 2, peer_all(j))
        return carry

    lax.fori_loop(1, total, send_sum, 0)

    decay = learning_rate * momentum_decay
    ufull[s, :key_rows] = (kw[...] - decay * km[...]).astype(bf16)
    ufull[s, key_rows:] = (rw[...] - decay * rm[...]).astype(bf16)
    for j in range(1, n_shard):
        put(ufull.at[s], ufull.at[s], 3, (d, lax.rem(s + j, n_shard)))

    wait_recv(nrecv.at[pl.ds(0, n_dp - 1)], 1)
    norm_sum = jnp.sum(nrecv[...].astype(f32), axis=0)
    nsum[...] = norm_sum
    norm_velocity, norm_master = advance(packed(nm[...]), packed(nw[...]), norm_sum / n_dp)
    npar[s] = norm_master.astype(bf16)
    for j in range(1, n_shard):
        put(npar.at[s], npar.at[s], 4, (d, lax.rem(s + j, n_shard)))

    wait_recv(recv2.at[pl.ds(0, total - 1)], 2)

    both = 2 * rank
    rows = jnp.concatenate(
        [recv2[n_dp * k : n_dp * (k + 1)].reshape(both, LANES) for k in range(n_shard)], axis=1
    )
    down = lax.broadcasted_iota(jnp.int32, (both, both), 0)
    along = lax.broadcasted_iota(jnp.int32, (both, both), 1)
    gram = lax.dot_general(rows, rows, nt, precision=highest, preferred_element_type=f32)
    gram = jnp.where((down < rank) == (along < rank), gram, 0.0)
    identity = jnp.where(down == along, 1.0, 0.0).astype(f32)
    square = gram * gram
    scale_key = jnp.sqrt(jnp.sum(square[:rank], keepdims=True)) + 1e-06
    scale_router = jnp.sqrt(jnp.sum(square[rank:], keepdims=True)) + 1e-06
    row_index = lax.broadcasted_iota(jnp.int32, (both, 1), 0)
    scaling = jnp.where(row_index < rank, scale_key, scale_router)

    def mul(a, b):
        return jnp.dot(a, b, precision=highest, preferred_element_type=f32)

    t = gram / scaling
    middle = 1.5 * identity - 0.5 * t
    root = middle
    for step in range(1, ROOT_STEPS):
        t = mul(t, 2.25 * identity - 1.5 * t + 0.25 * mul(t, t))
        middle = 1.5 * identity - 0.5 * t
        if step < ROOT_STEPS - 1:
            root = mul(middle, root)
    ortho[...] = mul(middle, mul(root, rows)) / jnp.sqrt(scaling)

    own = ortho[:, pl.ds(pl.multiple_of(s * LANES, LANES), LANES)]

    def columns_of(factor, merged):
        high, low = halves(factor)
        left = jnp.concatenate(
            [jnp.concatenate([high, high], axis=1), jnp.concatenate([low, low], axis=1)], axis=0
        )
        out = jnp.dot(left, merged, preferred_element_type=f32)
        return out[:rank] + out[rank:]

    part_key = columns_of(own[:rank], mk[...]).astype(bf16)
    part_router = columns_of(own[rank:, :router_rows], mr[...]).astype(bf16)
    for k in range(n_shard):
        part = part_key if k < n_shard // 2 else part_router
        top = 16 * (k % (n_shard // 2))
        for b in range(n_dp):
            at = (k % 2) * half + (k // 2) * n_dp + b
            csend[at] = part[top : top + 16, window(b) : window(b) + 3 * LANES]

    there = csend.at[pl.ds((1 - core) * half, half)]
    put(there, crecv, 5, (d, mate))
    wait_recv(crecv, 5)
    bsend[...] = (csend[pl.ds(core * half, half)].astype(f32) + crecv[...].astype(f32)).astype(bf16)

    def peer_core(j):
        to = lax.rem(q + j, half)
        return to, (lax.rem(to, n_dp), (to // n_dp) * 2 + core)

    def send_part(j, carry):
        to, device = peer_core(j)
        put(bsend.at[to], brecv.at[q], 6, device)
        return carry

    lax.fori_loop(1, half, send_part, 0)
    brecv[q] = bsend[q]
    wait_recv(brecv.at[pl.ds(0, half - 1)], 6)
    mine = core * half + q
    cols[mine] = (jnp.sum(brecv[...].astype(f32), axis=0) / n_dp).astype(bf16)

    def send_columns(j, carry):
        to, device = peer_core(j)
        put(cols.at[mine], cols.at[mine], 7, device)
        return carry

    lax.fori_loop(1, half, send_columns, 0)
    wait_recv(cols.at[pl.ds(0, half - 1)], 7)
    ours = cols.at[pl.ds(core * half, half)]
    put(ours, ours, 8, (d, mate))

    wait_recv(ufull.at[pl.ds(0, n_shard - 1)], 3)
    wait_recv(npar.at[pl.ds(0, n_shard - 1)], 4)
    wait_send(recv1.at[pl.ds(0, n_dp - 1)], 0)
    wait_send(nrecv.at[pl.ds(0, n_dp - 1)], 1)
    wait_send(recv2.at[pl.ds(0, total - 1)], 2)
    wait_send(ufull.at[pl.ds(0, n_shard - 1)], 3)
    wait_send(npar.at[pl.ds(0, n_shard - 1)], 4)
    wait_send(crecv, 5)
    wait_send(brecv.at[pl.ds(0, half - 1)], 6)
    wait_send(cols.at[pl.ds(0, half - 1)], 7)
    wait_recv(ours, 8)
    wait_send(ours, 8)


def finish_kernel(
    n_dp, n_shard, rank,
    kg, ke, rg, re, km, kw, rm, rw, nm, nw, ortho, cols, ufull, nsum, npar,
    key_carry, router_carry, key_velocity, key_master, key_params,
    router_velocity, router_master, router_params, norm_velocity, norm_master, norm_params,
    ck, cr,
):
    d = lax.axis_index("dp")
    s = lax.axis_index("shard")
    half = n_dp * n_shard // 2
    key_rows, router_rows = kg.shape[1], rg.shape[1]
    span = km.shape[1]
    for k in range(n_shard):
        where = ck if k < n_shard // 2 else cr
        top = 16 * (k % (n_shard // 2))
        for b in range(n_dp):
            at = (k % 2) * half + (k // 2) * n_dp + b
            skip = LANES if b % 2 else 0
            piece = cols[at][:, skip:]
            lane = window(b) + skip
            where[top : top + 16, lane : window(b) + 3 * LANES] = piece
            where[rank + top : rank + top + 16, lane : window(b) + 3 * LANES] = piece

    def turned(factor):
        return jnp.concatenate(halves(factor.T), axis=1)

    def dot(a, b):
        return jnp.dot(a, b, preferred_element_type=f32)

    own = ortho[:, pl.ds(pl.multiple_of(s * LANES, LANES), LANES)]
    own_key = turned(own[:rank])
    own_router = turned(own[rank:])[:router_rows]
    key_carry[0] = kg[0].astype(f32) + ke[0] - dot(own_key, ck[...])
    router_carry[0] = rg[0].astype(f32) + re[0] - dot(own_router, cr[...])

    def block(first):
        parts = []
        for k in (first, first + 1):
            parts.append(cols[(k % 2) * half + (k // 2) * n_dp + d].astype(f32))
        both = jnp.concatenate(parts, axis=0)
        extra = both.shape[1] - span
        picked = jnp.where(lax.rem(d, 2) == 1, both[:, extra:], both[:, :span]).astype(bf16)
        return jnp.concatenate([picked, picked], axis=0)

    block_key = block(0)
    block_router = block(n_shard // 2)
    key_velocity[...], key_master[...] = advance(km[...], kw[...], dot(own_key, block_key))
    router_velocity[...], router_master[...] = advance(
        rm[...], rw[...], dot(own_router, block_router)
    )
    for k in range(n_shard):
        factor = ortho[:, LANES * k : LANES * (k + 1)]
        approx = dot(turned(factor[:rank]), block_key)
        held = ufull[k].astype(f32)
        key_params[key_rows * k : key_rows * (k + 1)] = (
            held[:key_rows] - learning_rate * approx
        ).astype(bf16)
        approx = dot(turned(factor[rank:])[:router_rows], block_router)
        router_params[router_rows * k : router_rows * (k + 1)] = (
            held[key_rows:] - learning_rate * approx
        ).astype(bf16)

    pieces = nm.shape[1] // LANES

    def unpacked(x):
        return jnp.concatenate([x[2 * j : 2 * j + 2] for j in range(pieces)], axis=1)

    norm_velocity[...], norm_master[...] = advance(nm[...], nw[...], unpacked(nsum[...]) / n_dp)
    norm_params[...] = jnp.concatenate(
        [unpacked(npar[k].astype(f32)) for k in range(n_shard)], axis=1
    ).astype(bf16)


def fast_body(
    n_dp, n_shard,
    key_grad, key_error, router_grad, router_error, norm_grad, key_basis, router_basis,
    key_momentum, key_weight, router_momentum, router_weight, norm_momentum, norm_weight,
):
    rank, width = key_basis.shape
    key_rows, router_rows = key_grad.shape[1], router_grad.shape[1]
    span = key_momentum.shape[1]
    total, half = n_dp * n_shard, n_dp * n_shard // 2
    vmem = pl.BlockSpec(memory_space=pltpu.VMEM)
    shape = jax.ShapeDtypeStruct
    chunk = (16, 3 * LANES)
    middle = pl.pallas_call(
        functools.partial(exchange_kernel, n_dp, n_shard, rank),
        out_shape=[
            shape((2 * rank, n_shard * LANES), f32),
            shape((total,) + chunk, bf16),
            shape((n_shard, key_rows + router_rows, span), bf16),
            shape((16, LANES), f32),
            shape((n_shard, 16, LANES), bf16),
        ],
        in_specs=[vmem] * 13,
        out_specs=[vmem] * 5,
        scratch_shapes=[
            pltpu.VMEM((2 * key_rows, width), bf16),
            pltpu.VMEM((2 * router_rows, width), bf16),
            pltpu.VMEM((2 * rank, LANES), f32),
            pltpu.VMEM((n_dp, 8, LANES), f32),
            pltpu.VMEM((total, 8, LANES), f32),
            pltpu.VMEM((1, 16, LANES), bf16),
            pltpu.VMEM((n_dp, 16, LANES), bf16),
            pltpu.VMEM((total,) + chunk, bf16),
            pltpu.VMEM((half,) + chunk, bf16),
            pltpu.VMEM((half,) + chunk, bf16),
            pltpu.VMEM((half,) + chunk, bf16),
            pltpu.SemaphoreType.DMA((9,)),
            pltpu.SemaphoreType.DMA((9,)),
        ],
        compiler_params=pltpu.CompilerParams(
            collective_id=0, has_side_effects=True, vmem_limit_bytes=32 * 2**20
        ),
        name="exchange",
    )(
        key_grad, key_error, router_grad, router_error, norm_grad, key_basis, router_basis,
        key_momentum, key_weight, router_momentum, router_weight, norm_momentum, norm_weight,
    )
    return pl.pallas_call(
        functools.partial(finish_kernel, n_dp, n_shard, rank),
        out_shape=[
            shape(key_error.shape, f32),
            shape(router_error.shape, f32),
            shape(key_momentum.shape, f32),
            shape(key_momentum.shape, f32),
            shape((n_shard * key_rows, span), bf16),
            shape(router_momentum.shape, f32),
            shape(router_momentum.shape, f32),
            shape((n_shard * router_rows, span), bf16),
            shape(norm_momentum.shape, f32),
            shape(norm_momentum.shape, f32),
            shape((norm_momentum.shape[0], width), bf16),
        ],
        in_specs=[vmem] * 15,
        out_specs=[vmem] * 11,
        scratch_shapes=[
            pltpu.VMEM((2 * rank, width), bf16),
            pltpu.VMEM((2 * rank, width), bf16),
        ],
        compiler_params=pltpu.CompilerParams(vmem_limit_bytes=32 * 2**20),
        name="finish",
    )(
        key_grad, key_error, router_grad, router_error, key_momentum, key_weight,
        router_momentum, router_weight, norm_momentum, norm_weight, *middle,
    )


def solution(mesh):
    n_dp, n_shard = mesh.shape["dp"], mesh.shape["shard"]

    def body(*arrays):
        key_grad, router_grad, key_basis = arrays[0], arrays[2], arrays[5]
        rank, width = key_basis.shape
        tiled = (
            2 * rank == 8 * n_dp == 16 * n_shard
            and key_grad.shape[1] == LANES
            and router_grad.shape[1] == 16
            and 2 * width == 5 * LANES * n_dp
            and arrays[11].shape == (2, 5 * LANES)
        )
        if tiled:
            return fast_body(n_dp, n_shard, *arrays)
        return general_body(*arrays)

    return jax.shard_map(
        body,
        mesh=mesh,
        in_specs=(
            P("dp", "shard", None),
            P("dp", "shard", None),
            P("dp", "shard", None),
            P("dp", "shard", None),
            P("dp", None, "shard"),
            P(),
            P(),
            P("shard", "dp"),
            P("shard", "dp"),
            P("shard", "dp"),
            P("shard", "dp"),
            P(None, "shard"),
            P(None, "shard"),
        ),
        out_specs=(
            P("dp", "shard", None),
            P("dp", "shard", None),
            P("shard", "dp"),
            P("shard", "dp"),
            P(None, "dp"),
            P("shard", "dp"),
            P("shard", "dp"),
            P(None, "dp"),
            P(None, "shard"),
            P(None, "shard"),
            P(),
        ),
        check_vma=False,
    )
```

```python
import functools

import jax
import jax.numpy as jnp
from jax import lax
from jax.experimental import pallas as pl
from jax.experimental.pallas import tpu as pltpu
from jax.sharding import PartitionSpec as P

ROOT_STEPS = 4
MESH = pl.DeviceIdType.MESH
LANES = 128

highest = lax.Precision.HIGHEST
momentum_decay = 0.9
learning_rate = 0.1
f32 = jnp.float32
bf16 = jnp.bfloat16


def inverse_root(gram_matrix):
    scaling = jnp.sqrt(jnp.sum(gram_matrix * gram_matrix)) + 1e-06
    identity = jnp.eye(gram_matrix.shape[0], dtype=jnp.float32)
    square_side = gram_matrix / scaling
    root_side = identity
    for sweep_index in range(ROOT_STEPS):
        middle = 1.5 * identity - 0.5 * jnp.dot(root_side, square_side, precision=highest)
        square_side = jnp.dot(square_side, middle, precision=highest)
        root_side = jnp.dot(middle, root_side, precision=highest)
    return (root_side, scaling)


def project(old_basis, merged):
    return lax.dot_general(old_basis, merged, (((1,), (1,)), ((), ())), precision=highest)


def gram_of(factor_rows):
    return lax.dot_general(factor_rows, factor_rows, (((1,), (1,)), ((), ())), precision=highest)


def normalize(gram_matrix, factor_rows):
    root_side, scaling = inverse_root(gram_matrix)
    return jnp.dot(root_side, factor_rows, precision=highest) / jnp.sqrt(scaling)


def advance(momentum, weight, direction):
    velocity = momentum_decay * momentum + direction
    return (velocity, weight - learning_rate * velocity)


def general_body(
    key_grad,
    key_error,
    router_grad,
    router_error,
    norm_grad,
    key_basis,
    router_basis,
    key_momentum,
    key_weight,
    router_momentum,
    router_weight,
    norm_momentum,
    norm_weight,
):
    replicas = lax.axis_size("dp")
    rank_size = key_basis.shape[0]
    merged_key = key_grad[0].astype(jnp.float32) + key_error[0]
    merged_router = router_grad[0].astype(jnp.float32) + router_error[0]
    rows_key, rows_router, norm_sum = lax.psum(
        (
            project(key_basis, merged_key),
            project(router_basis, merged_router),
            norm_grad[0].astype(jnp.float32),
        ),
        "dp",
    )
    gram_key, gram_router = lax.psum((gram_of(rows_key), gram_of(rows_router)), "shard")
    ortho_key = normalize(gram_key, rows_key)
    ortho_router = normalize(gram_router, rows_router)
    key_part = lax.dot_general(merged_key, ortho_key, (((0,), (1,)), ((), ())), precision=highest)
    router_part = lax.dot_general(
        merged_router, ortho_router, (((0,), (1,)), ((), ())), precision=highest
    )
    column_sum = lax.psum(jnp.concatenate([key_part, router_part], axis=1), ("dp", "shard"))
    columns = column_sum / replicas
    approx_key = lax.dot_general(
        ortho_key, columns[:, :rank_size], (((0,), (1,)), ((), ())), precision=highest
    )
    approx_router = lax.dot_general(
        ortho_router, columns[:, rank_size:], (((0,), (1,)), ((), ())), precision=highest
    )
    col_width = key_momentum.shape[1]
    offset = lax.axis_index("dp") * col_width
    key_velocity, key_master = advance(
        key_momentum, key_weight, lax.dynamic_slice_in_dim(approx_key, offset, col_width, 1)
    )
    router_velocity, router_master = advance(
        router_momentum,
        router_weight,
        lax.dynamic_slice_in_dim(approx_router, offset, col_width, 1),
    )
    norm_velocity, norm_master = advance(norm_momentum, norm_weight, norm_sum / replicas)
    key_params, router_params, norm_params = (
        lax.all_gather(key_master.astype(jnp.bfloat16), "shard", axis=0, tiled=True),
        lax.all_gather(router_master.astype(jnp.bfloat16), "shard", axis=0, tiled=True),
        lax.all_gather(norm_master.astype(jnp.bfloat16), "shard", axis=1, tiled=True),
    )
    key_carry = (merged_key - approx_key)[None]
    router_carry = (merged_router - approx_router)[None]
    return (
        key_carry,
        router_carry,
        key_velocity,
        key_master,
        key_params,
        router_velocity,
        router_master,
        router_params,
        norm_velocity,
        norm_master,
        norm_params,
    )


def halves(x):
    high = x.astype(bf16)
    return high, (x - high.astype(f32)).astype(bf16)


def fold(x, rows, cols):
    y = x[:rows] + x[rows:]
    return y[:, :cols] + y[:, cols:]


def tile_start(d):
    return (5 * d + 1) // 2


def packed(x):
    pieces = [x[:, LANES * j : LANES * (j + 1)] for j in range(x.shape[1] // LANES)]
    rows = 2 * len(pieces)
    return jnp.concatenate(pieces + [jnp.zeros((16 - rows, LANES), f32)], axis=0)


NT = (((1,), (1,)), ((), ()))


def dot(a, b):
    return jnp.dot(a, b, preferred_element_type=f32)


def dot_nt(a, b):
    return lax.dot_general(a, b, NT, preferred_element_type=f32)


def mul(a, b, product=dot):
    a_high, a_low = halves(a)
    b_high, b_low = halves(b)
    both = product(jnp.concatenate([a_high, a_low], axis=0), b_high)
    rows = a.shape[0]
    return both[:rows] + (both[rows:] + product(a_high, b_low))


def exchange_kernel(
    n_dp, n_shard, rank,
    kg_h, ke_h, rg_h, re_h, kb_h, rb_h, ng_h, nm_h, nw_h, km_h, kw_h, rm_h, rw_h,
    mk, mr, km, kw, rm, rw, nm, nw, ortho, cols, ukey, urouter, nsum, npar,
    kg, ke, rg, re, kb, rb, ng,
    mkm, mrm, p64, recv1, recv2, nsend, nrecv, csend, brecv, load, send, recv,
):
    d = lax.axis_index("dp")
    s = lax.axis_index("shard")
    total = n_dp * n_shard
    me = d * n_shard + s
    core = lax.rem(s, 2)
    x = s // 2
    mate = s + 1 - 2 * core
    half = total // 2
    q = x * n_dp + d
    key_rows = mk.shape[0] // 2
    router_rows = mr.shape[0] // 2
    tiles = csend.shape[0] // 2

    fetched = {}
    pairs = dict(
        kg=(kg_h, kg), ke=(ke_h, ke), kb=(kb_h, kb), rg=(rg_h, rg), re=(re_h, re), rb=(rb_h, rb),
        ng=(ng_h, ng), nm=(nm_h, nm), nw=(nw_h, nw), km=(km_h, km), kw=(kw_h, kw),
        rm=(rm_h, rm), rw=(rw_h, rw),
    )
    for index, (name, (there, here)) in enumerate(pairs.items()):
        fetched[name] = pltpu.make_async_copy(there, here, load.at[index])
        fetched[name].start()

    def need(*names):
        for name in names:
            fetched[name].wait()

    def peer_all(j):
        t = lax.rem(me + j, total)
        return (t // n_shard, lax.rem(t, n_shard))

    barrier = pltpu.get_barrier_semaphore()

    def greet(j, carry):
        pl.semaphore_signal(barrier, inc=1, device_id=peer_all(j), device_id_type=MESH)
        return carry

    lax.fori_loop(1, total, greet, 0)

    def put(src, dst, which, device):
        pltpu.make_async_remote_copy(
            src_ref=src, dst_ref=dst, send_sem=send.at[which], recv_sem=recv.at[which],
            device_id=device, device_id_type=MESH,
        ).start()

    def wait_recv(ref, which):
        pltpu.make_async_copy(ref, ref, recv.at[which]).wait()

    def wait_send(ref, which):
        pltpu.make_async_copy(ref, ref, send.at[which]).wait()

    need("kg", "ke")
    high, low = halves(kg[0].astype(f32) + ke[0])
    mk[:key_rows] = high
    mk[key_rows:] = low
    need("kb")
    kb2 = jnp.concatenate(halves(kb[...]), axis=0)
    p64[:rank] = fold(dot_nt(kb2, mk[...]), rank, key_rows)
    need("rg", "re", "rb")
    high, low = halves(rg[0].astype(f32) + re[0])
    mr[:router_rows] = high
    mr[router_rows:] = low
    rb2 = jnp.concatenate(halves(rb[...]), axis=0)
    p64[rank:] = jnp.concatenate(
        [
            fold(dot_nt(rb2, mr[...]), rank, router_rows),
            jnp.zeros((rank, LANES - router_rows), f32),
        ],
        axis=1,
    )
    need("ng")
    nsend[0] = packed(ng[0].astype(f32)).astype(bf16)

    pl.semaphore_wait(barrier, total - 1)

    def send_rows(j, carry):
        t = lax.rem(d + j, n_dp)
        put(p64.at[pl.ds(pl.multiple_of(t * 8, 8), 8)], recv1.at[d], 0, (t, s))
        return carry

    lax.fori_loop(1, n_dp, send_rows, 0)

    def send_norm(j, carry):
        t = lax.rem(d + j, n_dp)
        put(nsend.at[0], nrecv.at[d], 1, (t, s))
        return carry

    lax.fori_loop(1, n_dp, send_norm, 0)

    @pl.when(core == 1)
    def _():
        put(mk, mkm, 5, (d, mate))

    @pl.when(core == 0)
    def _():
        put(mr, mrm, 5, (d, mate))

    recv1[d] = p64[pl.ds(pl.multiple_of(d * 8, 8), 8), :]
    nrecv[d] = nsend[0]
    wait_recv(recv1.at[pl.ds(0, n_dp - 1)], 0)
    slot = s * n_dp + d
    recv2[slot] = jnp.sum(recv1[...], axis=0)

    def send_sum(j, carry):
        put(recv2.at[slot], recv2.at[slot], 2, peer_all(j))
        return carry

    lax.fori_loop(1, total, send_sum, 0)

    decay = learning_rate * momentum_decay
    need("km", "kw", "rm", "rw")
    ukey[s] = (kw[...] - decay * km[...]).astype(bf16)
    urouter[s] = (rw[...] - decay * rm[...]).astype(bf16)
    for j in range(1, n_shard):
        to = (d, lax.rem(s + j, n_shard))
        put(ukey.at[s], ukey.at[s], 3, to)
        put(urouter.at[s], urouter.at[s], 9, to)

    need("nm", "nw")
    wait_recv(nrecv.at[pl.ds(0, n_dp - 1)], 1)
    norm_sum = jnp.sum(nrecv[...].astype(f32), axis=0)
    nsum[...] = norm_sum
    norm_velocity, norm_master = advance(packed(nm[...]), packed(nw[...]), norm_sum / n_dp)
    npar[s] = norm_master.astype(bf16)
    for j in range(1, n_shard):
        put(npar.at[s], npar.at[s], 4, (d, lax.rem(s + j, n_shard)))

    wait_recv(recv2.at[pl.ds(0, total - 1)], 2)

    both = 2 * rank
    rows = jnp.concatenate(
        [recv2[n_dp * k : n_dp * (k + 1)].reshape(both, LANES) for k in range(n_shard)], axis=1
    )
    down = lax.broadcasted_iota(jnp.int32, (both, both), 0)
    along = lax.broadcasted_iota(jnp.int32, (both, both), 1)
    gram = jnp.where((down < rank) == (along < rank), mul(rows, rows, dot_nt), 0.0)
    identity = jnp.where(down == along, 1.0, 0.0).astype(f32)
    square = gram * gram
    scale_key = jnp.sqrt(jnp.sum(square[:rank], keepdims=True)) + 1e-06
    scale_router = jnp.sqrt(jnp.sum(square[rank:], keepdims=True)) + 1e-06
    row_index = lax.broadcasted_iota(jnp.int32, (both, 1), 0)
    scaling = jnp.where(row_index < rank, scale_key, scale_router)
    t = gram / scaling
    middle = 1.5 * identity - 0.5 * t
    root = middle
    for step in range(1, ROOT_STEPS):
        t = mul(t, 2.25 * identity - 1.5 * t + 0.25 * mul(t, t))
        middle = 1.5 * identity - 0.5 * t
        if step < ROOT_STEPS - 1:
            root = mul(middle, root)
    ortho[...] = mul(middle, mul(root, rows)) / jnp.sqrt(scaling)

    def factor(which):
        return ortho[:, pl.ds(pl.multiple_of(which * LANES, LANES), LANES)]

    def columns_of(factor, merged):
        high, low = halves(factor)
        left = jnp.concatenate(
            [jnp.concatenate([high, high], axis=1), jnp.concatenate([low, low], axis=1)], axis=0
        )
        out = dot(left, merged)
        return out[:rank] + out[rank:]

    def keep(part):
        part = part.astype(bf16)
        for k in range(2):
            for j in range(tiles):
                csend[k * tiles + j] = part[16 * k : 16 * k + 16, LANES * j : LANES * (j + 1)]

    @pl.when(core == 0)
    def _():
        wait_recv(mkm, 5)
        keep(columns_of(factor(s)[:rank], mk[...]) + columns_of(factor(mate)[:rank], mkm[...]))

    @pl.when(core == 1)
    def _():
        wait_recv(mrm, 5)
        keep(
            columns_of(factor(s)[rank:, :router_rows], mr[...])
            + columns_of(factor(mate)[rank:, :router_rows], mrm[...])
        )

    def peer_core(j):
        to = lax.rem(q + j, half)
        return to // n_dp, lax.rem(to, n_dp)

    def send_part(j, carry):
        to_x, to_d = peer_core(j)
        first = to_x * tiles + tile_start(to_d)
        for parity, count in ((0, 3), (1, 2)):

            @pl.when(lax.rem(to_d, 2) == parity)
            def _():
                put(
                    csend.at[pl.ds(first, count)], brecv.at[q, pl.ds(0, count)], 6,
                    (to_d, to_x * 2 + core),
                )

        return carry

    lax.fori_loop(1, half, send_part, 0)
    offset = x * tiles + tile_start(d)
    mine = core * 2 * tiles + offset
    for parity, count in ((0, 3), (1, 2)):

        @pl.when(lax.rem(d, 2) == parity)
        def _():
            brecv[q, :count] = csend[pl.ds(offset, count)]
            wait_recv(cols.at[pl.ds(0, (half - 1) * count)], 6)
            added = jnp.sum(brecv[:, :count].astype(f32), axis=0) / n_dp
            cols[pl.ds(mine, count)] = added.astype(bf16)

            def send_columns(j, carry):
                to_x, to_d = peer_core(j)
                there = cols.at[pl.ds(mine, count)]
                put(there, there, 7, (to_d, to_x * 2 + core))
                return carry

            lax.fori_loop(1, half, send_columns, 0)
            wait_recv(cols.at[pl.ds(0, 2 * tiles - count)], 7)

    ours = cols.at[pl.ds(core * 2 * tiles, 2 * tiles)]
    put(ours, ours, 8, (d, mate))

    wait_recv(ukey.at[pl.ds(0, n_shard - 1)], 3)
    wait_recv(urouter.at[pl.ds(0, n_shard - 1)], 9)
    wait_recv(npar.at[pl.ds(0, n_shard - 1)], 4)
    wait_send(recv1.at[pl.ds(0, n_dp - 1)], 0)
    wait_send(nrecv.at[pl.ds(0, n_dp - 1)], 1)
    wait_send(recv2.at[pl.ds(0, total - 1)], 2)
    wait_send(ukey.at[pl.ds(0, n_shard - 1)], 3)
    wait_send(urouter.at[pl.ds(0, n_shard - 1)], 9)
    wait_send(npar.at[pl.ds(0, n_shard - 1)], 4)

    @pl.when(core == 1)
    def _():
        wait_send(mk, 5)

    @pl.when(core == 0)
    def _():
        wait_send(mr, 5)

    for parity, count in ((0, 3), (1, 2)):

        @pl.when(lax.rem(d, 2) == parity)
        def _():
            wait_send(csend.at[pl.ds(0, 2 * tiles - count)], 6)
            wait_send(cols.at[pl.ds(0, (half - 1) * count)], 7)

    wait_recv(ours, 8)
    wait_send(ours, 8)


def finish_kernel(
    n_dp, n_shard, rank,
    mk, mr, km, kw, rm, rw, nm, nw, ortho, cols, ukey, urouter, nsum, npar,
    key_carry, router_carry, key_velocity, key_master, key_params,
    router_velocity, router_master, router_params, norm_velocity, norm_master, norm_params,
    ck, cr,
):
    d = lax.axis_index("dp")
    s = lax.axis_index("shard")
    key_rows, router_rows = mk.shape[0] // 2, mr.shape[0] // 2
    span = km.shape[0]
    tiles = cols.shape[0] // 4
    for core, where in ((0, ck), (1, cr)):
        for k in range(2):
            for j in range(tiles):
                piece = cols[(core * 2 + k) * tiles + j]
                lanes = slice(LANES * j, LANES * (j + 1))
                where[16 * k : 16 * k + 16, lanes] = piece
                where[rank + 16 * k : rank + 16 * k + 16, lanes] = piece

    def turned(factor):
        return jnp.concatenate(halves(factor.T), axis=1)

    own = ortho[:, pl.ds(pl.multiple_of(s * LANES, LANES), LANES)]
    own_key = turned(own[:rank])
    own_router = turned(own[rank:])[:router_rows]
    merged = mk[:key_rows].astype(f32) + mk[key_rows:].astype(f32)
    key_carry[0] = merged - dot(own_key, ck[...])
    merged = mr[:router_rows].astype(f32) + mr[router_rows:].astype(f32)
    router_carry[0] = merged - dot(own_router, cr[...])

    def block(core):
        parts = []
        for k in range(2):
            near = cols[pl.ds((core * 2 + k) * tiles + 5 * d // 2, 3)].astype(f32)
            parts.append(jnp.concatenate([near[0], near[1], near[2]], axis=1))
        both = jnp.concatenate(parts, axis=0)
        extra = both.shape[1] - span
        return jnp.where(lax.rem(d, 2) == 1, both[:, extra:], both[:, :span])

    turned_block = block(0).T.astype(bf16)
    key_block = jnp.concatenate([turned_block, turned_block], axis=1)
    router_block = block(1).astype(bf16)
    router_block = jnp.concatenate([router_block, router_block], axis=0)
    key_velocity[...], key_master[...] = advance(
        km[...], kw[...], dot(key_block, jnp.concatenate(halves(own[:rank]), axis=0))
    )
    router_velocity[...], router_master[...] = advance(
        rm[...], rw[...], dot(own_router, router_block)
    )
    approx = dot(key_block, jnp.concatenate(halves(ortho[:rank]), axis=0))
    for k in range(n_shard):
        lanes = slice(key_rows * k, key_rows * (k + 1))
        key_params[:, lanes] = (
            ukey[k].astype(f32) - learning_rate * approx[:, lanes]
        ).astype(bf16)
        factor = turned(ortho[rank:, LANES * k : LANES * (k + 1)])[:router_rows]
        router_params[router_rows * k : router_rows * (k + 1)] = (
            urouter[k].astype(f32) - learning_rate * dot(factor, router_block)
        ).astype(bf16)

    pieces = nm.shape[1] // LANES

    def unpacked(x):
        return jnp.concatenate([x[2 * j : 2 * j + 2] for j in range(pieces)], axis=1)

    norm_velocity[...], norm_master[...] = advance(nm[...], nw[...], unpacked(nsum[...]) / n_dp)
    norm_params[...] = jnp.concatenate(
        [unpacked(npar[k].astype(f32)) for k in range(n_shard)], axis=1
    ).astype(bf16)


def fast_body(
    n_dp, n_shard,
    key_grad, key_error, router_grad, router_error, norm_grad, key_basis, router_basis,
    key_momentum, key_weight, router_momentum, router_weight, norm_momentum, norm_weight,
):
    rank, width = key_basis.shape
    key_rows, router_rows = key_grad.shape[1], router_grad.shape[1]
    span = key_momentum.shape[1]
    total, half, tiles = n_dp * n_shard, n_dp * n_shard // 2, width // LANES
    vmem = pl.BlockSpec(memory_space=pltpu.VMEM)
    hbm = pl.BlockSpec(memory_space=pltpu.HBM)
    shape = jax.ShapeDtypeStruct
    key_state, router_state = shape((span, key_rows), f32), shape((router_rows, span), f32)
    norm_state = shape(norm_momentum.shape, f32)
    middle = pl.pallas_call(
        functools.partial(exchange_kernel, n_dp, n_shard, rank),
        out_shape=[
            shape((2 * key_rows, width), bf16),
            shape((2 * router_rows, width), bf16),
            key_state,
            key_state,
            router_state,
            router_state,
            norm_state,
            norm_state,
            shape((2 * rank, n_shard * LANES), f32),
            shape((4 * tiles, 16, LANES), bf16),
            shape((n_shard, span, key_rows), bf16),
            shape((n_shard, router_rows, span), bf16),
            shape((16, LANES), f32),
            shape((n_shard, 16, LANES), bf16),
        ],
        in_specs=[hbm] * 13,
        out_specs=[vmem] * 14,
        scratch_shapes=[
            pltpu.VMEM(key_grad.shape, bf16),
            pltpu.VMEM(key_error.shape, f32),
            pltpu.VMEM(router_grad.shape, bf16),
            pltpu.VMEM(router_error.shape, f32),
            pltpu.VMEM(key_basis.shape, f32),
            pltpu.VMEM(router_basis.shape, f32),
            pltpu.VMEM(norm_grad.shape, bf16),
            pltpu.VMEM((2 * key_rows, width), bf16),
            pltpu.VMEM((2 * router_rows, width), bf16),
            pltpu.VMEM((2 * rank, LANES), f32),
            pltpu.VMEM((n_dp, 8, LANES), f32),
            pltpu.VMEM((total, 8, LANES), f32),
            pltpu.VMEM((1, 16, LANES), bf16),
            pltpu.VMEM((n_dp, 16, LANES), bf16),
            pltpu.VMEM((2 * tiles, 16, LANES), bf16),
            pltpu.VMEM((half, 3, 16, LANES), bf16),
            pltpu.SemaphoreType.DMA((13,)),
            pltpu.SemaphoreType.DMA((10,)),
            pltpu.SemaphoreType.DMA((10,)),
        ],
        compiler_params=pltpu.CompilerParams(
            collective_id=0, has_side_effects=True, vmem_limit_bytes=24 * 2**20
        ),
        name="exchange",
    )(
        *(
            pltpu.with_memory_space_constraint(operand, pltpu.HBM)
            for operand in (
                key_grad, key_error, router_grad, router_error, key_basis, router_basis, norm_grad,
                norm_momentum, norm_weight, key_momentum.T, key_weight.T, router_momentum,
                router_weight,
            )
        )
    )
    results = pl.pallas_call(
        functools.partial(finish_kernel, n_dp, n_shard, rank),
        out_shape=[
            shape(key_error.shape, f32),
            shape(router_error.shape, f32),
            key_state,
            key_state,
            shape((span, n_shard * key_rows), bf16),
            router_state,
            router_state,
            shape((n_shard * router_rows, span), bf16),
            norm_state,
            norm_state,
            shape((norm_momentum.shape[0], width), bf16),
        ],
        in_specs=[vmem] * 14,
        out_specs=[vmem] * 11,
        scratch_shapes=[
            pltpu.VMEM((2 * rank, width), bf16),
            pltpu.VMEM((2 * rank, width), bf16),
        ],
        compiler_params=pltpu.CompilerParams(vmem_limit_bytes=24 * 2**20),
        name="finish",
    )(*middle)
    return tuple(y.T if i in (2, 3, 4) else y for i, y in enumerate(results))


def solution(mesh):
    n_dp, n_shard = mesh.shape["dp"], mesh.shape["shard"]

    def body(*arrays):
        key_grad, router_grad, key_basis = arrays[0], arrays[2], arrays[5]
        rank, width = key_basis.shape
        tiled = (
            2 * rank == 8 * n_dp == 16 * n_shard
            and key_grad.shape[1] == LANES
            and router_grad.shape[1] == 16
            and 2 * width == 5 * LANES * n_dp
            and arrays[11].shape == (2, 5 * LANES)
        )
        if tiled:
            return fast_body(n_dp, n_shard, *arrays)
        return general_body(*arrays)

    return jax.shard_map(
        body,
        mesh=mesh,
        in_specs=(
            P("dp", "shard", None),
            P("dp", "shard", None),
            P("dp", "shard", None),
            P("dp", "shard", None),
            P("dp", None, "shard"),
            P(),
            P(),
            P("shard", "dp"),
            P("shard", "dp"),
            P("shard", "dp"),
            P("shard", "dp"),
            P(None, "shard"),
            P(None, "shard"),
        ),
        out_specs=(
            P("dp", "shard", None),
            P("dp", "shard", None),
            P("shard", "dp"),
            P("shard", "dp"),
            P(None, "dp"),
            P("shard", "dp"),
            P("shard", "dp"),
            P(None, "dp"),
            P(None, "shard"),
            P(None, "shard"),
            P(),
        ),
        check_vma=False,
    )
```

```python
import functools

import jax
import jax.numpy as jnp
from jax import lax
from jax.experimental import pallas as pl
from jax.experimental.pallas import tpu as pltpu
from jax.sharding import PartitionSpec as P

ROOT_STEPS = 4
MESH = pl.DeviceIdType.MESH
LANES = 128

highest = lax.Precision.HIGHEST
momentum_decay = 0.9
learning_rate = 0.1
f32 = jnp.float32
bf16 = jnp.bfloat16


def inverse_root(gram_matrix):
    scaling = jnp.sqrt(jnp.sum(gram_matrix * gram_matrix)) + 1e-06
    identity = jnp.eye(gram_matrix.shape[0], dtype=jnp.float32)
    square_side = gram_matrix / scaling
    root_side = identity
    for sweep_index in range(ROOT_STEPS):
        middle = 1.5 * identity - 0.5 * jnp.dot(root_side, square_side, precision=highest)
        square_side = jnp.dot(square_side, middle, precision=highest)
        root_side = jnp.dot(middle, root_side, precision=highest)
    return (root_side, scaling)


def project(old_basis, merged):
    return lax.dot_general(old_basis, merged, (((1,), (1,)), ((), ())), precision=highest)


def gram_of(factor_rows):
    return lax.dot_general(factor_rows, factor_rows, (((1,), (1,)), ((), ())), precision=highest)


def normalize(gram_matrix, factor_rows):
    root_side, scaling = inverse_root(gram_matrix)
    return jnp.dot(root_side, factor_rows, precision=highest) / jnp.sqrt(scaling)


def advance(momentum, weight, direction):
    velocity = momentum_decay * momentum + direction
    return (velocity, weight - learning_rate * velocity)


def general_body(
    key_grad,
    key_error,
    router_grad,
    router_error,
    norm_grad,
    key_basis,
    router_basis,
    key_momentum,
    key_weight,
    router_momentum,
    router_weight,
    norm_momentum,
    norm_weight,
):
    replicas = lax.axis_size("dp")
    rank_size = key_basis.shape[0]
    merged_key = key_grad[0].astype(jnp.float32) + key_error[0]
    merged_router = router_grad[0].astype(jnp.float32) + router_error[0]
    rows_key, rows_router, norm_sum = lax.psum(
        (
            project(key_basis, merged_key),
            project(router_basis, merged_router),
            norm_grad[0].astype(jnp.float32),
        ),
        "dp",
    )
    gram_key, gram_router = lax.psum((gram_of(rows_key), gram_of(rows_router)), "shard")
    ortho_key = normalize(gram_key, rows_key)
    ortho_router = normalize(gram_router, rows_router)
    key_part = lax.dot_general(merged_key, ortho_key, (((0,), (1,)), ((), ())), precision=highest)
    router_part = lax.dot_general(
        merged_router, ortho_router, (((0,), (1,)), ((), ())), precision=highest
    )
    column_sum = lax.psum(jnp.concatenate([key_part, router_part], axis=1), ("dp", "shard"))
    columns = column_sum / replicas
    approx_key = lax.dot_general(
        ortho_key, columns[:, :rank_size], (((0,), (1,)), ((), ())), precision=highest
    )
    approx_router = lax.dot_general(
        ortho_router, columns[:, rank_size:], (((0,), (1,)), ((), ())), precision=highest
    )
    col_width = key_momentum.shape[1]
    offset = lax.axis_index("dp") * col_width
    key_velocity, key_master = advance(
        key_momentum, key_weight, lax.dynamic_slice_in_dim(approx_key, offset, col_width, 1)
    )
    router_velocity, router_master = advance(
        router_momentum,
        router_weight,
        lax.dynamic_slice_in_dim(approx_router, offset, col_width, 1),
    )
    norm_velocity, norm_master = advance(norm_momentum, norm_weight, norm_sum / replicas)
    key_params, router_params, norm_params = (
        lax.all_gather(key_master.astype(jnp.bfloat16), "shard", axis=0, tiled=True),
        lax.all_gather(router_master.astype(jnp.bfloat16), "shard", axis=0, tiled=True),
        lax.all_gather(norm_master.astype(jnp.bfloat16), "shard", axis=1, tiled=True),
    )
    key_carry = (merged_key - approx_key)[None]
    router_carry = (merged_router - approx_router)[None]
    return (
        key_carry,
        router_carry,
        key_velocity,
        key_master,
        key_params,
        router_velocity,
        router_master,
        router_params,
        norm_velocity,
        norm_master,
        norm_params,
    )


def halves(x):
    high = x.astype(bf16)
    return high, (x - high.astype(f32)).astype(bf16)


def fold(x, rows, cols):
    y = x[:rows] + x[rows:]
    return y[:, :cols] + y[:, cols:]


def tile_start(d):
    return (5 * d + 1) // 2


def packed(x):
    pieces = [x[:, LANES * j : LANES * (j + 1)] for j in range(x.shape[1] // LANES)]
    rows = 2 * len(pieces)
    return jnp.concatenate(pieces + [jnp.zeros((16 - rows, LANES), f32)], axis=0)


NT = (((1,), (1,)), ((), ()))


def dot(a, b):
    return jnp.dot(a, b, preferred_element_type=f32)


def dot_nt(a, b):
    return lax.dot_general(a, b, NT, preferred_element_type=f32)


def mul(a, b, product=dot):
    a_high, a_low = halves(a)
    b_high, b_low = halves(b)
    both = product(jnp.concatenate([a_high, a_low], axis=0), b_high)
    rows = a.shape[0]
    return both[:rows] + (both[rows:] + product(a_high, b_low))


def exchange_kernel(
    n_dp, n_shard, rank,
    kg_h, ke_h, rg_h, re_h, kb_h, rb_h, ng_h, nm_h, nw_h, km_h, kw_h, rm_h, rw_h,
    mk, mr, km, kw, rm, rw, nm, nw, ortho, cols, ukey, urouter, nsum, npar,
    kg, ke, rg, re, kb, rb, ng,
    mkm, mrm, p64, recv1, recv2, nsend, nrecv, csend, brecv, load, send, recv,
):
    d = lax.axis_index("dp")
    s = lax.axis_index("shard")
    total = n_dp * n_shard
    me = d * n_shard + s
    core = lax.rem(s, 2)
    x = s // 2
    mate = s + 1 - 2 * core
    half = total // 2
    q = x * n_dp + d
    key_rows = mk.shape[0] // 2
    router_rows = mr.shape[0] // 2
    tiles = csend.shape[0] // 2

    pairs = n_dp // 2
    span = mk.shape[1] // pairs
    chunks = [slice(span * p, span * (p + 1)) for p in range(pairs)]
    fetched = {}

    def fetch(name, there, here):
        fetched[name] = pltpu.make_async_copy(there, here, load.at[len(fetched)])
        fetched[name].start()

    def need(*names):
        for name in names:
            fetched[name].wait()

    fetch("rg", rg_h, rg)
    fetch("re", re_h, re)
    fetch("rb", rb_h, rb)
    for p, lanes in enumerate(chunks):
        fetch(("kg", p), kg_h.at[:, :, lanes], kg.at[:, :, lanes])
        fetch(("ke", p), ke_h.at[:, :, lanes], ke.at[:, :, lanes])
        fetch(("kb", p), kb_h.at[:, lanes], kb.at[:, lanes])
    fetch("ng", ng_h, ng)
    fetch("km", km_h, km)
    fetch("kw", kw_h, kw)
    fetch("rm", rm_h, rm)
    fetch("rw", rw_h, rw)
    fetch("nm", nm_h, nm)
    fetch("nw", nw_h, nw)

    def peer_all(j):
        t = lax.rem(me + j, total)
        return (t // n_shard, lax.rem(t, n_shard))

    barrier = pltpu.get_barrier_semaphore()

    def greet(j, carry):
        pl.semaphore_signal(barrier, inc=1, device_id=peer_all(j), device_id_type=MESH)
        return carry

    lax.fori_loop(1, total, greet, 0)

    def put(src, dst, which, device):
        pltpu.make_async_remote_copy(
            src_ref=src, dst_ref=dst, send_sem=send.at[which], recv_sem=recv.at[which],
            device_id=device, device_id_type=MESH,
        ).start()

    def wait_recv(ref, which):
        pltpu.make_async_copy(ref, ref, recv.at[which]).wait()

    def wait_send(ref, which):
        pltpu.make_async_copy(ref, ref, send.at[which]).wait()

    need("rg", "re", "rb")
    high, low = halves(rg[0].astype(f32) + re[0])
    mr[:router_rows] = high
    mr[router_rows:] = low
    rb2 = jnp.concatenate(halves(rb[...]), axis=0)
    p64[rank:] = jnp.concatenate(
        [
            fold(dot_nt(rb2, mr[...]), rank, router_rows),
            jnp.zeros((rank, LANES - router_rows), f32),
        ],
        axis=1,
    )
    projected = None
    for p, lanes in enumerate(chunks):
        need(("kg", p), ("ke", p), ("kb", p))
        high, low = halves(kg[0, :, lanes].astype(f32) + ke[0, :, lanes])
        mk[:key_rows, lanes] = high
        mk[key_rows:, lanes] = low
        kb2 = jnp.concatenate(halves(kb[:, lanes]), axis=0)
        term = dot_nt(kb2, jnp.concatenate([high, low], axis=0))
        projected = term if projected is None else projected + term
    p64[:rank] = fold(projected, rank, key_rows)

    pl.semaphore_wait(barrier, total - 1)

    def far_first(count):
        return sorted(range(1, count), key=lambda j: -min(j, count - j))

    for j in far_first(n_dp):
        to = lax.rem(d + j, n_dp)
        put(p64.at[pl.ds(pl.multiple_of(to * 8, 8), 8)], recv1.at[d], 0, (to, s))
    recv1[d] = p64[pl.ds(pl.multiple_of(d * 8, 8), 8), :]
    need("ng")
    nsend[0] = packed(ng[0].astype(f32)).astype(bf16)
    nrecv[d] = nsend[0]
    need("km", "kw", "rm", "rw")
    decay = learning_rate * momentum_decay
    ukey[s] = (kw[...] - decay * km[...]).astype(bf16)
    urouter[s] = (rw[...] - decay * rm[...]).astype(bf16)
    wait_recv(recv1.at[pl.ds(0, n_dp - 1)], 0)
    slot = s * n_dp + d
    recv2[slot] = jnp.sum(recv1[...], axis=0)
    for j in far_first(total):
        put(recv2.at[slot], recv2.at[slot], 2, peer_all(j))

    @pl.when(core == 1)
    def _():
        put(mk, mkm, 5, (d, mate))

    @pl.when(core == 0)
    def _():
        put(mr, mrm, 5, (d, mate))

    for j in range(1, n_dp):
        put(nsend.at[0], nrecv.at[d], 1, (lax.rem(d + j, n_dp), s))

    wait_recv(recv2.at[pl.ds(0, total - 1)], 2)

    for j in range(1, n_shard):
        to = (d, lax.rem(s + j, n_shard))
        put(ukey.at[s], ukey.at[s], 3, to)
        put(urouter.at[s], urouter.at[s], 9, to)

    both = 2 * rank
    rows = jnp.concatenate(
        [recv2[n_dp * k : n_dp * (k + 1)].reshape(both, LANES) for k in range(n_shard)], axis=1
    )
    down = lax.broadcasted_iota(jnp.int32, (both, both), 0)
    along = lax.broadcasted_iota(jnp.int32, (both, both), 1)
    gram = jnp.where((down < rank) == (along < rank), mul(rows, rows, dot_nt), 0.0)
    identity = jnp.where(down == along, 1.0, 0.0).astype(f32)
    square = gram * gram
    scale_key = jnp.sqrt(jnp.sum(square[:rank], keepdims=True)) + 1e-06
    scale_router = jnp.sqrt(jnp.sum(square[rank:], keepdims=True)) + 1e-06
    row_index = lax.broadcasted_iota(jnp.int32, (both, 1), 0)
    scaling = jnp.where(row_index < rank, scale_key, scale_router)
    t = gram / scaling
    middle = 1.5 * identity - 0.5 * t
    root = middle
    for step in range(1, ROOT_STEPS):
        t = mul(t, 2.25 * identity - 1.5 * t + 0.25 * mul(t, t))
        middle = 1.5 * identity - 0.5 * t
        if step < ROOT_STEPS - 1:
            root = mul(middle, root)
    ortho[...] = mul(middle, mul(root, rows)) / jnp.sqrt(scaling)

    def factor(which):
        return ortho[:, pl.ds(pl.multiple_of(which * LANES, LANES), LANES)]

    def stacked(factor):
        high, low = halves(factor)
        return jnp.concatenate(
            [jnp.concatenate([high, high], axis=1), jnp.concatenate([low, low], axis=1)], axis=0
        )

    per_pair = tiles // pairs

    def columns_of(owner, left_own, own_ref, left_mate, mate_ref):
        for step in (2, 1, 3, 0):
            p = lax.rem(d // 2 + step, pairs)
            lanes = pl.ds(pl.multiple_of(p * span, LANES), span)
            out = dot(left_own, own_ref[:, lanes]) + dot(left_mate, mate_ref[:, lanes])
            part = (out[:rank] + out[rank:]).astype(bf16)
            for k in range(2):
                for j in range(per_pair):
                    csend[k * tiles + per_pair * p + j] = part[
                        16 * k : 16 * k + 16, LANES * j : LANES * (j + 1)
                    ]
            for k in range(2):
                for odd, first, count in ((0, 0, 3), (1, 3, 2)):
                    to_d = 2 * p + odd

                    def send_part():
                        put(
                            csend.at[pl.ds(k * tiles + per_pair * p + first, count)],
                            brecv.at[q, pl.ds(0, count)], 6, (to_d, 2 * k + owner),
                        )

                    if step:
                        send_part()
                    else:
                        pl.when(jnp.logical_or(x != k, to_d != d))(send_part)

    @pl.when(core == 0)
    def _():
        own, other = stacked(factor(s)[:rank]), stacked(factor(mate)[:rank])
        wait_recv(mkm, 5)
        columns_of(0, own, mk, other, mkm)

    @pl.when(core == 1)
    def _():
        own = stacked(factor(s)[rank:, :router_rows])
        other = stacked(factor(mate)[rank:, :router_rows])
        wait_recv(mrm, 5)
        columns_of(1, own, mr, other, mrm)

    need("nm", "nw")
    wait_recv(nrecv.at[pl.ds(0, n_dp - 1)], 1)
    norm_sum = jnp.sum(nrecv[...].astype(f32), axis=0)
    nsum[...] = norm_sum
    norm_velocity, norm_master = advance(packed(nm[...]), packed(nw[...]), norm_sum / n_dp)
    npar[s] = norm_master.astype(bf16)
    for j in range(1, n_shard):
        put(npar.at[s], npar.at[s], 4, (d, lax.rem(s + j, n_shard)))

    def peer_core(j):
        to = lax.rem(q + j, half)
        return to // n_dp, lax.rem(to, n_dp)

    offset = x * tiles + tile_start(d)
    mine = core * 2 * tiles + offset
    for parity, count in ((0, 3), (1, 2)):

        @pl.when(lax.rem(d, 2) == parity)
        def _():
            brecv[q, :count] = csend[pl.ds(offset, count)]
            wait_recv(cols.at[pl.ds(0, (half - 1) * count)], 6)
            added = jnp.sum(brecv[:, :count].astype(f32), axis=0) / n_dp
            cols[pl.ds(mine, count)] = added.astype(bf16)

            there = cols.at[pl.ds(mine, count)]
            for j in far_first(half):
                to_x, to_d = peer_core(j)
                put(there, there, 7 + 3 * lax.rem(to_x + x, 2), (to_d, to_x * 2 + core))
            wait_recv(cols.at[pl.ds(0, tiles - count)], 7)

    ours = cols.at[pl.ds(core * 2 * tiles + x * tiles, tiles)]
    put(ours, ours, 8, (d, mate))
    theirs = cols.at[pl.ds(core * 2 * tiles + (1 - x) * tiles, tiles)]
    wait_recv(theirs, 10)
    put(theirs, theirs, 11, (d, mate))

    wait_recv(ukey.at[pl.ds(0, n_shard - 1)], 3)
    wait_recv(urouter.at[pl.ds(0, n_shard - 1)], 9)
    wait_recv(npar.at[pl.ds(0, n_shard - 1)], 4)
    wait_send(recv1.at[pl.ds(0, n_dp - 1)], 0)
    wait_send(nrecv.at[pl.ds(0, n_dp - 1)], 1)
    wait_send(recv2.at[pl.ds(0, total - 1)], 2)
    wait_send(ukey.at[pl.ds(0, n_shard - 1)], 3)
    wait_send(urouter.at[pl.ds(0, n_shard - 1)], 9)
    wait_send(npar.at[pl.ds(0, n_shard - 1)], 4)

    @pl.when(core == 1)
    def _():
        wait_send(mk, 5)

    @pl.when(core == 0)
    def _():
        wait_send(mr, 5)

    for parity, count in ((0, 3), (1, 2)):

        @pl.when(lax.rem(d, 2) == parity)
        def _():
            wait_send(csend.at[pl.ds(0, 2 * tiles - count)], 6)
            wait_send(cols.at[pl.ds(0, (n_dp - 1) * count)], 7)
            wait_send(cols.at[pl.ds(0, n_dp * count)], 10)

    wait_send(ours, 8)
    wait_send(theirs, 11)
    wait_recv(ours, 8)
    wait_recv(theirs, 11)


def finish_kernel(
    n_dp, n_shard, rank,
    mk, mr, km, kw, rm, rw, nm, nw, ortho, cols, ukey, urouter, nsum, npar,
    key_carry, router_carry, key_velocity, key_master, key_params,
    router_velocity, router_master, router_params, norm_velocity, norm_master, norm_params,
    carry, out,
):
    d = lax.axis_index("dp")
    s = lax.axis_index("shard")
    key_rows, router_rows = mk.shape[0] // 2, mr.shape[0] // 2
    span = km.shape[0]
    tiles = cols.shape[0] // 4
    pairs = n_dp // 2
    per_pair = tiles // pairs

    def columns(core, p):
        parts = [
            jnp.concatenate(
                [cols[(core * 2 + k) * tiles + per_pair * p + j] for j in range(per_pair)], axis=1
            )
            for k in range(2)
        ]
        return jnp.concatenate(parts + parts, axis=0)

    def turned(factor):
        return jnp.concatenate(halves(factor.T), axis=1)

    own = ortho[:, pl.ds(pl.multiple_of(s * LANES, LANES), LANES)]
    own_key = turned(own[:rank])
    own_router = turned(own[rank:])[:router_rows]
    copies = []
    for p in range(pairs):
        lanes = slice(LANES * per_pair * p, LANES * per_pair * (p + 1))
        merged = mk[:key_rows, lanes].astype(f32) + mk[key_rows:, lanes].astype(f32)
        carry[0, :, lanes] = merged - dot(own_key, columns(0, p))
        copies.append(
            pltpu.make_async_copy(
                carry.at[:, :, lanes], key_carry.at[:, :, lanes], out.at[p]
            )
        )
        copies[-1].start()
        merged = mr[:router_rows, lanes].astype(f32) + mr[router_rows:, lanes].astype(f32)
        router_carry[0, :, lanes] = merged - dot(own_router, columns(1, p))

    def block(core):
        parts = []
        for k in range(2):
            near = cols[pl.ds((core * 2 + k) * tiles + 5 * d // 2, 3)].astype(f32)
            parts.append(jnp.concatenate([near[0], near[1], near[2]], axis=1))
        both = jnp.concatenate(parts, axis=0)
        extra = both.shape[1] - span
        return jnp.where(lax.rem(d, 2) == 1, both[:, extra:], both[:, :span])

    turned_block = block(0).T.astype(bf16)
    key_block = jnp.concatenate([turned_block, turned_block], axis=1)
    router_block = block(1).astype(bf16)
    router_block = jnp.concatenate([router_block, router_block], axis=0)
    key_velocity[...], key_master[...] = advance(
        km[...], kw[...], dot(key_block, jnp.concatenate(halves(own[:rank]), axis=0))
    )
    router_velocity[...], router_master[...] = advance(
        rm[...], rw[...], dot(own_router, router_block)
    )
    approx = dot(key_block, jnp.concatenate(halves(ortho[:rank]), axis=0))
    for k in range(n_shard):
        lanes = slice(key_rows * k, key_rows * (k + 1))
        key_params[:, lanes] = (
            ukey[k].astype(f32) - learning_rate * approx[:, lanes]
        ).astype(bf16)
        factor = turned(ortho[rank:, LANES * k : LANES * (k + 1)])[:router_rows]
        router_params[router_rows * k : router_rows * (k + 1)] = (
            urouter[k].astype(f32) - learning_rate * dot(factor, router_block)
        ).astype(bf16)

    pieces = nm.shape[1] // LANES

    def unpacked(x):
        return jnp.concatenate([x[2 * j : 2 * j + 2] for j in range(pieces)], axis=1)

    norm_velocity[...], norm_master[...] = advance(nm[...], nw[...], unpacked(nsum[...]) / n_dp)
    norm_params[...] = jnp.concatenate(
        [unpacked(npar[k].astype(f32)) for k in range(n_shard)], axis=1
    ).astype(bf16)
    for copy in copies:
        copy.wait()


def fast_body(
    n_dp, n_shard,
    key_grad, key_error, router_grad, router_error, norm_grad, key_basis, router_basis,
    key_momentum, key_weight, router_momentum, router_weight, norm_momentum, norm_weight,
):
    rank, width = key_basis.shape
    key_rows, router_rows = key_grad.shape[1], router_grad.shape[1]
    span = key_momentum.shape[1]
    total, half, tiles = n_dp * n_shard, n_dp * n_shard // 2, width // LANES
    vmem = pl.BlockSpec(memory_space=pltpu.VMEM)
    hbm = pl.BlockSpec(memory_space=pltpu.HBM)
    shape = jax.ShapeDtypeStruct
    key_state, router_state = shape((span, key_rows), f32), shape((router_rows, span), f32)
    norm_state = shape(norm_momentum.shape, f32)
    middle = pl.pallas_call(
        functools.partial(exchange_kernel, n_dp, n_shard, rank),
        out_shape=[
            shape((2 * key_rows, width), bf16),
            shape((2 * router_rows, width), bf16),
            key_state,
            key_state,
            router_state,
            router_state,
            norm_state,
            norm_state,
            shape((2 * rank, n_shard * LANES), f32),
            shape((4 * tiles, 16, LANES), bf16),
            shape((n_shard, span, key_rows), bf16),
            shape((n_shard, router_rows, span), bf16),
            shape((16, LANES), f32),
            shape((n_shard, 16, LANES), bf16),
        ],
        in_specs=[hbm] * 13,
        out_specs=[vmem] * 14,
        scratch_shapes=[
            pltpu.VMEM(key_grad.shape, bf16),
            pltpu.VMEM(key_error.shape, f32),
            pltpu.VMEM(router_grad.shape, bf16),
            pltpu.VMEM(router_error.shape, f32),
            pltpu.VMEM(key_basis.shape, f32),
            pltpu.VMEM(router_basis.shape, f32),
            pltpu.VMEM(norm_grad.shape, bf16),
            pltpu.VMEM((2 * key_rows, width), bf16),
            pltpu.VMEM((2 * router_rows, width), bf16),
            pltpu.VMEM((2 * rank, LANES), f32),
            pltpu.VMEM((n_dp, 8, LANES), f32),
            pltpu.VMEM((total, 8, LANES), f32),
            pltpu.VMEM((1, 16, LANES), bf16),
            pltpu.VMEM((n_dp, 16, LANES), bf16),
            pltpu.VMEM((2 * tiles, 16, LANES), bf16),
            pltpu.VMEM((half, 3, 16, LANES), bf16),
            pltpu.SemaphoreType.DMA((10 + 3 * n_dp // 2,)),
            pltpu.SemaphoreType.DMA((12,)),
            pltpu.SemaphoreType.DMA((12,)),
        ],
        compiler_params=pltpu.CompilerParams(
            collective_id=0, has_side_effects=True, vmem_limit_bytes=24 * 2**20
        ),
        name="exchange",
    )(
        *(
            pltpu.with_memory_space_constraint(operand, pltpu.HBM)
            for operand in (
                key_grad, key_error, router_grad, router_error, key_basis, router_basis, norm_grad,
                norm_momentum, norm_weight, key_momentum.T, key_weight.T, router_momentum,
                router_weight,
            )
        )
    )
    results = pl.pallas_call(
        functools.partial(finish_kernel, n_dp, n_shard, rank),
        out_shape=[
            shape(key_error.shape, f32),
            shape(router_error.shape, f32),
            key_state,
            key_state,
            shape((span, n_shard * key_rows), bf16),
            router_state,
            router_state,
            shape((n_shard * router_rows, span), bf16),
            norm_state,
            norm_state,
            shape((norm_momentum.shape[0], width), bf16),
        ],
        in_specs=[vmem] * 14,
        out_specs=[hbm] + [vmem] * 10,
        scratch_shapes=[
            pltpu.VMEM(key_error.shape, f32),
            pltpu.SemaphoreType.DMA((n_dp // 2,)),
        ],
        compiler_params=pltpu.CompilerParams(vmem_limit_bytes=24 * 2**20),
        name="finish",
    )(*middle)
    return tuple(y.T if i in (2, 3, 4) else y for i, y in enumerate(results))


def solution(mesh):
    n_dp, n_shard = mesh.shape["dp"], mesh.shape["shard"]

    def body(*arrays):
        key_grad, router_grad, key_basis = arrays[0], arrays[2], arrays[5]
        rank, width = key_basis.shape
        tiled = (
            2 * rank == 8 * n_dp == 16 * n_shard
            and key_grad.shape[1] == LANES
            and router_grad.shape[1] == 16
            and 2 * width == 5 * LANES * n_dp
            and arrays[11].shape == (2, 5 * LANES)
        )
        if tiled:
            return fast_body(n_dp, n_shard, *arrays)
        return general_body(*arrays)

    return jax.shard_map(
        body,
        mesh=mesh,
        in_specs=(
            P("dp", "shard", None),
            P("dp", "shard", None),
            P("dp", "shard", None),
            P("dp", "shard", None),
            P("dp", None, "shard"),
            P(),
            P(),
            P("shard", "dp"),
            P("shard", "dp"),
            P("shard", "dp"),
            P("shard", "dp"),
            P(None, "shard"),
            P(None, "shard"),
        ),
        out_specs=(
            P("dp", "shard", None),
            P("dp", "shard", None),
            P("shard", "dp"),
            P("shard", "dp"),
            P(None, "dp"),
            P("shard", "dp"),
            P("shard", "dp"),
            P(None, "dp"),
            P(None, "shard"),
            P(None, "shard"),
            P(),
        ),
        check_vma=False,
    )
```

```python
import functools

import jax
import jax.numpy as jnp
from jax import lax
from jax.experimental import pallas as pl
from jax.experimental.pallas import tpu as pltpu
from jax.sharding import PartitionSpec as P

ROOT_STEPS = 4
MESH = pl.DeviceIdType.MESH
LANES = 128

highest = lax.Precision.HIGHEST
momentum_decay = 0.9
learning_rate = 0.1
f32 = jnp.float32
bf16 = jnp.bfloat16


def inverse_root(gram_matrix):
    scaling = jnp.sqrt(jnp.sum(gram_matrix * gram_matrix)) + 1e-06
    identity = jnp.eye(gram_matrix.shape[0], dtype=jnp.float32)
    square_side = gram_matrix / scaling
    root_side = identity
    for sweep_index in range(ROOT_STEPS):
        middle = 1.5 * identity - 0.5 * jnp.dot(root_side, square_side, precision=highest)
        square_side = jnp.dot(square_side, middle, precision=highest)
        root_side = jnp.dot(middle, root_side, precision=highest)
    return (root_side, scaling)


def project(old_basis, merged):
    return lax.dot_general(old_basis, merged, (((1,), (1,)), ((), ())), precision=highest)


def gram_of(factor_rows):
    return lax.dot_general(factor_rows, factor_rows, (((1,), (1,)), ((), ())), precision=highest)


def normalize(gram_matrix, factor_rows):
    root_side, scaling = inverse_root(gram_matrix)
    return jnp.dot(root_side, factor_rows, precision=highest) / jnp.sqrt(scaling)


def advance(momentum, weight, direction):
    velocity = momentum_decay * momentum + direction
    return (velocity, weight - learning_rate * velocity)


def general_body(
    key_grad,
    key_error,
    router_grad,
    router_error,
    norm_grad,
    key_basis,
    router_basis,
    key_momentum,
    key_weight,
    router_momentum,
    router_weight,
    norm_momentum,
    norm_weight,
):
    replicas = lax.axis_size("dp")
    rank_size = key_basis.shape[0]
    merged_key = key_grad[0].astype(jnp.float32) + key_error[0]
    merged_router = router_grad[0].astype(jnp.float32) + router_error[0]
    rows_key, rows_router, norm_sum = lax.psum(
        (
            project(key_basis, merged_key),
            project(router_basis, merged_router),
            norm_grad[0].astype(jnp.float32),
        ),
        "dp",
    )
    gram_key, gram_router = lax.psum((gram_of(rows_key), gram_of(rows_router)), "shard")
    ortho_key = normalize(gram_key, rows_key)
    ortho_router = normalize(gram_router, rows_router)
    key_part = lax.dot_general(merged_key, ortho_key, (((0,), (1,)), ((), ())), precision=highest)
    router_part = lax.dot_general(
        merged_router, ortho_router, (((0,), (1,)), ((), ())), precision=highest
    )
    column_sum = lax.psum(jnp.concatenate([key_part, router_part], axis=1), ("dp", "shard"))
    columns = column_sum / replicas
    approx_key = lax.dot_general(
        ortho_key, columns[:, :rank_size], (((0,), (1,)), ((), ())), precision=highest
    )
    approx_router = lax.dot_general(
        ortho_router, columns[:, rank_size:], (((0,), (1,)), ((), ())), precision=highest
    )
    col_width = key_momentum.shape[1]
    offset = lax.axis_index("dp") * col_width
    key_velocity, key_master = advance(
        key_momentum, key_weight, lax.dynamic_slice_in_dim(approx_key, offset, col_width, 1)
    )
    router_velocity, router_master = advance(
        router_momentum,
        router_weight,
        lax.dynamic_slice_in_dim(approx_router, offset, col_width, 1),
    )
    norm_velocity, norm_master = advance(norm_momentum, norm_weight, norm_sum / replicas)
    key_params, router_params, norm_params = (
        lax.all_gather(key_master.astype(jnp.bfloat16), "shard", axis=0, tiled=True),
        lax.all_gather(router_master.astype(jnp.bfloat16), "shard", axis=0, tiled=True),
        lax.all_gather(norm_master.astype(jnp.bfloat16), "shard", axis=1, tiled=True),
    )
    key_carry = (merged_key - approx_key)[None]
    router_carry = (merged_router - approx_router)[None]
    return (
        key_carry,
        router_carry,
        key_velocity,
        key_master,
        key_params,
        router_velocity,
        router_master,
        router_params,
        norm_velocity,
        norm_master,
        norm_params,
    )


def halves(x):
    high = x.astype(bf16)
    return high, (x - high.astype(f32)).astype(bf16)


def fold(x, rows, cols):
    y = x[:rows] + x[rows:]
    return y[:, :cols] + y[:, cols:]


def tile_start(d):
    return (5 * d + 1) // 2


def packed(x):
    pieces = [x[:, LANES * j : LANES * (j + 1)] for j in range(x.shape[1] // LANES)]
    rows = 2 * len(pieces)
    return jnp.concatenate(pieces + [jnp.zeros((16 - rows, LANES), f32)], axis=0)


NT = (((1,), (1,)), ((), ()))


def dot(a, b):
    return jnp.dot(a, b, preferred_element_type=f32)


def dot_nt(a, b):
    return lax.dot_general(a, b, NT, preferred_element_type=f32)


def mul(a, b, product=dot):
    a_high, a_low = halves(a)
    b_high, b_low = halves(b)
    both = product(jnp.concatenate([a_high, a_low], axis=0), b_high)
    rows = a.shape[0]
    return both[:rows] + (both[rows:] + product(a_high, b_low))


def exchange_kernel(
    n_dp, n_shard, rank,
    kg_h, ke_h, rg_h, re_h, kb_h, rb_h, ng_h, nm_h, nw_h, km_h, kw_h, rm_h, rw_h,
    mk, mr, km, kw, rm, rw, nm, nw, lift, cols, ukey, urouter, nsum, npar,
    kg, ke, rg, re, kb, rb, ng,
    mkm, mrm, p64, recv1, recv2, nsend, nrecv, csend, brecv, load, send, recv,
):
    d = lax.axis_index("dp")
    s = lax.axis_index("shard")
    total = n_dp * n_shard
    me = d * n_shard + s
    core = lax.rem(s, 2)
    x = s // 2
    mate = s + 1 - 2 * core
    half = total // 2
    q = x * n_dp + d
    key_rows = mk.shape[0] // 2
    router_rows = mr.shape[0] // 2
    tiles = csend.shape[0] // 2

    pairs = n_dp // 2
    span = mk.shape[1] // pairs
    chunks = [slice(span * p, span * (p + 1)) for p in range(pairs)]
    fetched = {}

    def fetch(name, there, here):
        fetched[name] = pltpu.make_async_copy(there, here, load.at[len(fetched)])
        fetched[name].start()

    def need(*names):
        for name in names:
            fetched[name].wait()

    fetch("rg", rg_h, rg)
    fetch("re", re_h, re)
    fetch("rb", rb_h, rb)
    for p, lanes in enumerate(chunks):
        fetch(("kg", p), kg_h.at[:, :, lanes], kg.at[:, :, lanes])
        fetch(("ke", p), ke_h.at[:, :, lanes], ke.at[:, :, lanes])
        fetch(("kb", p), kb_h.at[:, lanes], kb.at[:, lanes])
    fetch("ng", ng_h, ng)
    fetch("km", km_h, km)
    fetch("kw", kw_h, kw)
    fetch("rm", rm_h, rm)
    fetch("rw", rw_h, rw)
    fetch("nm", nm_h, nm)
    fetch("nw", nw_h, nw)

    def peer_all(j):
        t = lax.rem(me + j, total)
        return (t // n_shard, lax.rem(t, n_shard))

    barrier = pltpu.get_barrier_semaphore()

    def greet(j, carry):
        pl.semaphore_signal(barrier, inc=1, device_id=peer_all(j), device_id_type=MESH)
        return carry

    lax.fori_loop(1, total, greet, 0)

    def put(src, dst, which, device):
        pltpu.make_async_remote_copy(
            src_ref=src, dst_ref=dst, send_sem=send.at[which], recv_sem=recv.at[which],
            device_id=device, device_id_type=MESH,
        ).start()

    def wait_recv(ref, which):
        pltpu.make_async_copy(ref, ref, recv.at[which]).wait()

    def wait_send(ref, which):
        pltpu.make_async_copy(ref, ref, send.at[which]).wait()

    need("rg", "re", "rb")
    high, low = halves(rg[0].astype(f32) + re[0])
    mr[:router_rows] = high
    mr[router_rows:] = low
    mrm[:router_rows] = high
    rb2 = jnp.concatenate(halves(rb[...]), axis=0)
    p64[rank:] = jnp.concatenate(
        [
            fold(dot_nt(rb2, mr[...]), rank, router_rows),
            jnp.zeros((rank, LANES - router_rows), f32),
        ],
        axis=1,
    )
    projected = None
    for p, lanes in enumerate(chunks):
        need(("kg", p), ("ke", p), ("kb", p))
        high, low = halves(kg[0, :, lanes].astype(f32) + ke[0, :, lanes])
        mk[:key_rows, lanes] = high
        mk[key_rows:, lanes] = low
        mkm[:key_rows, lanes] = high
        kb2 = jnp.concatenate(halves(kb[:, lanes]), axis=0)
        term = dot_nt(kb2, jnp.concatenate([high, low], axis=0))
        projected = term if projected is None else projected + term
    p64[:rank] = fold(projected, rank, key_rows)

    pl.semaphore_wait(barrier, total - 1)

    def far_first(count):
        return sorted(range(1, count), key=lambda j: -min(j, count - j))

    for j in far_first(n_dp):
        to = lax.rem(d + j, n_dp)
        put(p64.at[pl.ds(pl.multiple_of(to * 8, 8), 8)], recv1.at[d], 0, (to, s))

    key_half, router_half = pl.ds(key_rows, key_rows), pl.ds(router_rows, router_rows)

    @pl.when(core == 1)
    def _():
        put(mk.at[pl.ds(0, key_rows)], mkm.at[key_half], 5, (d, mate))

    @pl.when(core == 0)
    def _():
        put(mr.at[pl.ds(0, router_rows)], mrm.at[router_half], 5, (d, mate))

    recv1[d] = p64[pl.ds(pl.multiple_of(d * 8, 8), 8), :]
    need("ng")
    nsend[0] = packed(ng[0].astype(f32)).astype(bf16)
    nrecv[d] = nsend[0]
    need("km", "kw", "rm", "rw")
    decay = learning_rate * momentum_decay
    ukey[s] = (kw[...] - decay * km[...]).astype(bf16)
    urouter[s] = (rw[...] - decay * rm[...]).astype(bf16)
    wait_recv(recv1.at[pl.ds(0, n_dp - 1)], 0)
    slot = s * n_dp + d
    recv2[slot] = jnp.sum(recv1[...], axis=0)
    summed = recv2.at[slot]
    for j in far_first(n_dp):
        put(summed, summed, 2, (lax.rem(d + j, n_dp), s))
    for j in far_first(n_dp) + [0]:
        put(summed, summed, 2, (lax.rem(d + j, n_dp), mate))
    for j in far_first(n_dp) + [0]:
        for other in range(2):
            put(summed, summed, 12, (lax.rem(d + j, n_dp), 2 * (1 - x) + other))

    for j in range(1, n_dp):
        put(nsend.at[0], nrecv.at[d], 1, (lax.rem(d + j, n_dp), s))

    for j in range(1, n_shard):
        to = (d, lax.rem(s + j, n_shard))
        put(ukey.at[s], ukey.at[s], 3, to)
        put(urouter.at[s], urouter.at[s], 9, to)

    wait_recv(recv2.at[pl.ds(0, half - 1)], 2)

    def factor(which, first):
        count = rank // 8
        return recv2[pl.ds(which * n_dp + first * count, count)].reshape(rank, LANES)

    def stacked(own, other):
        return jnp.concatenate(halves(jnp.concatenate([own, other], axis=1)), axis=0)

    per_pair = tiles // pairs

    def columns_of(owner, left, merged):
        for step in (2, 1, 3, 0):
            p = lax.rem(d // 2 + step, pairs)
            lanes = pl.ds(pl.multiple_of(p * span, LANES), span)
            out = dot(left, merged[:, lanes])
            part = (out[:rank] + out[rank:]).astype(bf16)
            for k in range(2):
                for j in range(per_pair):
                    csend[k * tiles + per_pair * p + j] = part[
                        16 * k : 16 * k + 16, LANES * j : LANES * (j + 1)
                    ]
            for k in range(2):
                for odd, first, count in ((0, 0, 3), (1, 3, 2)):
                    to_d = 2 * p + odd

                    def send_part():
                        put(
                            csend.at[pl.ds(k * tiles + per_pair * p + first, count)],
                            brecv.at[q, pl.ds(0, count)], 6, (to_d, 2 * k + owner),
                        )

                    if step:
                        send_part()
                    else:
                        pl.when(jnp.logical_or(x != k, to_d != d))(send_part)

    @pl.when(core == 0)
    def _():
        left = stacked(factor(s, 0), factor(mate, 0))
        wait_recv(mkm.at[key_half], 5)
        columns_of(0, left, mkm)

    @pl.when(core == 1)
    def _():
        left = stacked(factor(s, 1)[:, :router_rows], factor(mate, 1)[:, :router_rows])
        wait_recv(mrm.at[router_half], 5)
        columns_of(1, left, mrm)

    wait_recv(recv2.at[pl.ds(0, half)], 12)

    both = 2 * rank
    rows = jnp.concatenate(
        [recv2[n_dp * k : n_dp * (k + 1)].reshape(both, LANES) for k in range(n_shard)], axis=1
    )
    down = lax.broadcasted_iota(jnp.int32, (both, both), 0)
    along = lax.broadcasted_iota(jnp.int32, (both, both), 1)
    gram = jnp.where((down < rank) == (along < rank), mul(rows, rows, dot_nt), 0.0)
    identity = jnp.where(down == along, 1.0, 0.0).astype(f32)
    square = gram * gram
    scale_key = jnp.sqrt(jnp.sum(square[:rank], keepdims=True)) + 1e-06
    scale_router = jnp.sqrt(jnp.sum(square[rank:], keepdims=True)) + 1e-06
    row_index = lax.broadcasted_iota(jnp.int32, (both, 1), 0)
    scaling = jnp.where(row_index < rank, scale_key, scale_router)
    t = gram / scaling
    middle = 1.5 * identity - 0.5 * t
    root = middle
    for step in range(1, ROOT_STEPS):
        t = mul(t, 2.25 * identity - 1.5 * t + 0.25 * mul(t, t))
        middle = 1.5 * identity - 0.5 * t
        if step < ROOT_STEPS - 1:
            root = mul(middle, root)
    root = mul(middle, root)
    lift[...] = mul(root, mul(root, rows)) / scaling

    need("nm", "nw")
    wait_recv(nrecv.at[pl.ds(0, n_dp - 1)], 1)
    norm_sum = jnp.sum(nrecv[...].astype(f32), axis=0)
    nsum[...] = norm_sum
    norm_velocity, norm_master = advance(packed(nm[...]), packed(nw[...]), norm_sum / n_dp)
    npar[s] = norm_master.astype(bf16)
    for j in range(1, n_shard):
        put(npar.at[s], npar.at[s], 4, (d, lax.rem(s + j, n_shard)))

    def peer_core(j):
        to = lax.rem(q + j, half)
        return to // n_dp, lax.rem(to, n_dp)

    offset = x * tiles + tile_start(d)
    mine = core * 2 * tiles + offset
    for parity, count in ((0, 3), (1, 2)):

        @pl.when(lax.rem(d, 2) == parity)
        def _():
            brecv[q, :count] = csend[pl.ds(offset, count)]
            wait_recv(cols.at[pl.ds(0, (half - 1) * count)], 6)
            added = jnp.sum(brecv[:, :count].astype(f32), axis=0) / n_dp
            cols[pl.ds(mine, count)] = added.astype(bf16)

            there = cols.at[pl.ds(mine, count)]
            for j in far_first(half):
                to_x, to_d = peer_core(j)
                put(there, there, 7 + 3 * lax.rem(to_x + x, 2), (to_d, to_x * 2 + core))
            wait_recv(cols.at[pl.ds(0, tiles - count)], 7)

    ours = cols.at[pl.ds(core * 2 * tiles + x * tiles, tiles)]
    put(ours, ours, 8, (d, mate))
    theirs = cols.at[pl.ds(core * 2 * tiles + (1 - x) * tiles, tiles)]
    wait_recv(theirs, 10)
    put(theirs, theirs, 11, (d, mate))

    wait_recv(ukey.at[pl.ds(0, n_shard - 1)], 3)
    wait_recv(urouter.at[pl.ds(0, n_shard - 1)], 9)
    wait_recv(npar.at[pl.ds(0, n_shard - 1)], 4)
    wait_send(recv1.at[pl.ds(0, n_dp - 1)], 0)
    wait_send(nrecv.at[pl.ds(0, n_dp - 1)], 1)
    wait_send(recv2.at[pl.ds(0, half - 1)], 2)
    wait_send(recv2.at[pl.ds(0, half)], 12)
    wait_send(ukey.at[pl.ds(0, n_shard - 1)], 3)
    wait_send(urouter.at[pl.ds(0, n_shard - 1)], 9)
    wait_send(npar.at[pl.ds(0, n_shard - 1)], 4)

    @pl.when(core == 1)
    def _():
        wait_send(mkm.at[key_half], 5)

    @pl.when(core == 0)
    def _():
        wait_send(mrm.at[router_half], 5)

    for parity, count in ((0, 3), (1, 2)):

        @pl.when(lax.rem(d, 2) == parity)
        def _():
            wait_send(csend.at[pl.ds(0, 2 * tiles - count)], 6)
            wait_send(cols.at[pl.ds(0, (n_dp - 1) * count)], 7)
            wait_send(cols.at[pl.ds(0, n_dp * count)], 10)

    wait_send(ours, 8)
    wait_send(theirs, 11)
    wait_recv(ours, 8)
    wait_recv(theirs, 11)


def finish_kernel(
    n_dp, n_shard, rank,
    mk, mr, km, kw, rm, rw, nm, nw, lift, cols, ukey, urouter, nsum, npar,
    key_carry, router_carry, key_velocity, key_master, key_params,
    router_velocity, router_master, router_params, norm_velocity, norm_master, norm_params,
    ck, cr,
):
    d = lax.axis_index("dp")
    s = lax.axis_index("shard")
    key_rows, router_rows = mk.shape[0] // 2, mr.shape[0] // 2
    span = km.shape[0]
    tiles = cols.shape[0] // 4
    for core, where in ((0, ck), (1, cr)):
        for k in range(2):
            for j in range(tiles):
                piece = cols[(core * 2 + k) * tiles + j]
                lanes = slice(LANES * j, LANES * (j + 1))
                where[16 * k : 16 * k + 16, lanes] = piece
                where[rank + 16 * k : rank + 16 * k + 16, lanes] = piece

    def turned(factor):
        return jnp.concatenate(halves(factor.T), axis=1)

    own = lift[:, pl.ds(pl.multiple_of(s * LANES, LANES), LANES)]
    own_key = turned(own[:rank])
    own_router = turned(own[rank:])[:router_rows]
    merged = mk[:key_rows].astype(f32) + mk[key_rows:].astype(f32)
    key_carry[0] = merged - dot(own_key, ck[...])
    merged = mr[:router_rows].astype(f32) + mr[router_rows:].astype(f32)
    router_carry[0] = merged - dot(own_router, cr[...])

    def block(core):
        parts = []
        for k in range(2):
            near = cols[pl.ds((core * 2 + k) * tiles + 5 * d // 2, 3)].astype(f32)
            parts.append(jnp.concatenate([near[0], near[1], near[2]], axis=1))
        both = jnp.concatenate(parts, axis=0)
        extra = both.shape[1] - span
        return jnp.where(lax.rem(d, 2) == 1, both[:, extra:], both[:, :span])

    turned_block = block(0).T.astype(bf16)
    key_block = jnp.concatenate([turned_block, turned_block], axis=1)
    router_block = block(1).astype(bf16)
    router_block = jnp.concatenate([router_block, router_block], axis=0)
    key_velocity[...], key_master[...] = advance(
        km[...], kw[...], dot(key_block, jnp.concatenate(halves(own[:rank]), axis=0))
    )
    router_velocity[...], router_master[...] = advance(
        rm[...], rw[...], dot(own_router, router_block)
    )
    approx = dot(key_block, jnp.concatenate(halves(lift[:rank]), axis=0))
    for k in range(n_shard):
        lanes = slice(key_rows * k, key_rows * (k + 1))
        key_params[:, lanes] = (
            ukey[k].astype(f32) - learning_rate * approx[:, lanes]
        ).astype(bf16)
        factor = turned(lift[rank:, LANES * k : LANES * (k + 1)])[:router_rows]
        router_params[router_rows * k : router_rows * (k + 1)] = (
            urouter[k].astype(f32) - learning_rate * dot(factor, router_block)
        ).astype(bf16)

    pieces = nm.shape[1] // LANES

    def unpacked(x):
        return jnp.concatenate([x[2 * j : 2 * j + 2] for j in range(pieces)], axis=1)

    norm_velocity[...], norm_master[...] = advance(nm[...], nw[...], unpacked(nsum[...]) / n_dp)
    norm_params[...] = jnp.concatenate(
        [unpacked(npar[k].astype(f32)) for k in range(n_shard)], axis=1
    ).astype(bf16)


def fast_body(
    n_dp, n_shard,
    key_grad, key_error, router_grad, router_error, norm_grad, key_basis, router_basis,
    key_momentum, key_weight, router_momentum, router_weight, norm_momentum, norm_weight,
):
    rank, width = key_basis.shape
    key_rows, router_rows = key_grad.shape[1], router_grad.shape[1]
    span = key_momentum.shape[1]
    total, half, tiles = n_dp * n_shard, n_dp * n_shard // 2, width // LANES
    vmem = pl.BlockSpec(memory_space=pltpu.VMEM)
    hbm = pl.BlockSpec(memory_space=pltpu.HBM)
    shape = jax.ShapeDtypeStruct
    key_state, router_state = shape((span, key_rows), f32), shape((router_rows, span), f32)
    norm_state = shape(norm_momentum.shape, f32)
    middle = pl.pallas_call(
        functools.partial(exchange_kernel, n_dp, n_shard, rank),
        out_shape=[
            shape((2 * key_rows, width), bf16),
            shape((2 * router_rows, width), bf16),
            key_state,
            key_state,
            router_state,
            router_state,
            norm_state,
            norm_state,
            shape((2 * rank, n_shard * LANES), f32),
            shape((4 * tiles, 16, LANES), bf16),
            shape((n_shard, span, key_rows), bf16),
            shape((n_shard, router_rows, span), bf16),
            shape((16, LANES), f32),
            shape((n_shard, 16, LANES), bf16),
        ],
        in_specs=[hbm] * 13,
        out_specs=[vmem] * 14,
        scratch_shapes=[
            pltpu.VMEM(key_grad.shape, bf16),
            pltpu.VMEM(key_error.shape, f32),
            pltpu.VMEM(router_grad.shape, bf16),
            pltpu.VMEM(router_error.shape, f32),
            pltpu.VMEM(key_basis.shape, f32),
            pltpu.VMEM(router_basis.shape, f32),
            pltpu.VMEM(norm_grad.shape, bf16),
            pltpu.VMEM((2 * key_rows, width), bf16),
            pltpu.VMEM((2 * router_rows, width), bf16),
            pltpu.VMEM((2 * rank, LANES), f32),
            pltpu.VMEM((n_dp, 8, LANES), f32),
            pltpu.VMEM((total, 8, LANES), f32),
            pltpu.VMEM((1, 16, LANES), bf16),
            pltpu.VMEM((n_dp, 16, LANES), bf16),
            pltpu.VMEM((2 * tiles, 16, LANES), bf16),
            pltpu.VMEM((half, 3, 16, LANES), bf16),
            pltpu.SemaphoreType.DMA((10 + 3 * n_dp // 2,)),
            pltpu.SemaphoreType.DMA((13,)),
            pltpu.SemaphoreType.DMA((13,)),
        ],
        compiler_params=pltpu.CompilerParams(
            collective_id=0, has_side_effects=True, vmem_limit_bytes=24 * 2**20
        ),
        name="exchange",
    )(
        *(
            pltpu.with_memory_space_constraint(operand, pltpu.HBM)
            for operand in (
                key_grad, key_error, router_grad, router_error, key_basis, router_basis, norm_grad,
                norm_momentum, norm_weight, key_momentum.T, key_weight.T, router_momentum,
                router_weight,
            )
        )
    )
    results = pl.pallas_call(
        functools.partial(finish_kernel, n_dp, n_shard, rank),
        out_shape=[
            shape(key_error.shape, f32),
            shape(router_error.shape, f32),
            key_state,
            key_state,
            shape((span, n_shard * key_rows), bf16),
            router_state,
            router_state,
            shape((n_shard * router_rows, span), bf16),
            norm_state,
            norm_state,
            shape((norm_momentum.shape[0], width), bf16),
        ],
        in_specs=[vmem] * 14,
        out_specs=[vmem] * 11,
        scratch_shapes=[
            pltpu.VMEM((2 * rank, width), bf16),
            pltpu.VMEM((2 * rank, width), bf16),
        ],
        compiler_params=pltpu.CompilerParams(vmem_limit_bytes=24 * 2**20),
        name="finish",
    )(*middle)
    return tuple(y.T if i in (2, 3, 4) else y for i, y in enumerate(results))


def solution(mesh):
    n_dp, n_shard = mesh.shape["dp"], mesh.shape["shard"]

    def body(*arrays):
        key_grad, router_grad, key_basis = arrays[0], arrays[2], arrays[5]
        rank, width = key_basis.shape
        tiled = (
            2 * rank == 8 * n_dp == 16 * n_shard
            and key_grad.shape[1] == LANES
            and router_grad.shape[1] == 16
            and 2 * width == 5 * LANES * n_dp
            and arrays[11].shape == (2, 5 * LANES)
        )
        if tiled:
            return fast_body(n_dp, n_shard, *arrays)
        return general_body(*arrays)

    return jax.shard_map(
        body,
        mesh=mesh,
        in_specs=(
            P("dp", "shard", None),
            P("dp", "shard", None),
            P("dp", "shard", None),
            P("dp", "shard", None),
            P("dp", None, "shard"),
            P(),
            P(),
            P("shard", "dp"),
            P("shard", "dp"),
            P("shard", "dp"),
            P("shard", "dp"),
            P(None, "shard"),
            P(None, "shard"),
        ),
        out_specs=(
            P("dp", "shard", None),
            P("dp", "shard", None),
            P("shard", "dp"),
            P("shard", "dp"),
            P(None, "dp"),
            P("shard", "dp"),
            P("shard", "dp"),
            P(None, "dp"),
            P(None, "shard"),
            P(None, "shard"),
            P(),
        ),
        check_vma=False,
    )
```

```python
import functools

import jax
import jax.numpy as jnp
from jax import lax
from jax.experimental import pallas as pl
from jax.experimental.pallas import tpu as pltpu
from jax.sharding import PartitionSpec as P

ROOT_STEPS = 4
MESH = pl.DeviceIdType.MESH
LANES = 128

highest = lax.Precision.HIGHEST
momentum_decay = 0.9
learning_rate = 0.1
f32 = jnp.float32
bf16 = jnp.bfloat16


def inverse_root(gram_matrix):
    scaling = jnp.sqrt(jnp.sum(gram_matrix * gram_matrix)) + 1e-06
    identity = jnp.eye(gram_matrix.shape[0], dtype=jnp.float32)
    square_side = gram_matrix / scaling
    root_side = identity
    for sweep_index in range(ROOT_STEPS):
        middle = 1.5 * identity - 0.5 * jnp.dot(root_side, square_side, precision=highest)
        square_side = jnp.dot(square_side, middle, precision=highest)
        root_side = jnp.dot(middle, root_side, precision=highest)
    return (root_side, scaling)


def project(old_basis, merged):
    return lax.dot_general(old_basis, merged, (((1,), (1,)), ((), ())), precision=highest)


def gram_of(factor_rows):
    return lax.dot_general(factor_rows, factor_rows, (((1,), (1,)), ((), ())), precision=highest)


def normalize(gram_matrix, factor_rows):
    root_side, scaling = inverse_root(gram_matrix)
    return jnp.dot(root_side, factor_rows, precision=highest) / jnp.sqrt(scaling)


def advance(momentum, weight, direction):
    velocity = momentum_decay * momentum + direction
    return (velocity, weight - learning_rate * velocity)


def general_body(
    key_grad,
    key_error,
    router_grad,
    router_error,
    norm_grad,
    key_basis,
    router_basis,
    key_momentum,
    key_weight,
    router_momentum,
    router_weight,
    norm_momentum,
    norm_weight,
):
    replicas = lax.axis_size("dp")
    rank_size = key_basis.shape[0]
    merged_key = key_grad[0].astype(jnp.float32) + key_error[0]
    merged_router = router_grad[0].astype(jnp.float32) + router_error[0]
    rows_key, rows_router, norm_sum = lax.psum(
        (
            project(key_basis, merged_key),
            project(router_basis, merged_router),
            norm_grad[0].astype(jnp.float32),
        ),
        "dp",
    )
    gram_key, gram_router = lax.psum((gram_of(rows_key), gram_of(rows_router)), "shard")
    ortho_key = normalize(gram_key, rows_key)
    ortho_router = normalize(gram_router, rows_router)
    key_part = lax.dot_general(merged_key, ortho_key, (((0,), (1,)), ((), ())), precision=highest)
    router_part = lax.dot_general(
        merged_router, ortho_router, (((0,), (1,)), ((), ())), precision=highest
    )
    column_sum = lax.psum(jnp.concatenate([key_part, router_part], axis=1), ("dp", "shard"))
    columns = column_sum / replicas
    approx_key = lax.dot_general(
        ortho_key, columns[:, :rank_size], (((0,), (1,)), ((), ())), precision=highest
    )
    approx_router = lax.dot_general(
        ortho_router, columns[:, rank_size:], (((0,), (1,)), ((), ())), precision=highest
    )
    col_width = key_momentum.shape[1]
    offset = lax.axis_index("dp") * col_width
    key_velocity, key_master = advance(
        key_momentum, key_weight, lax.dynamic_slice_in_dim(approx_key, offset, col_width, 1)
    )
    router_velocity, router_master = advance(
        router_momentum,
        router_weight,
        lax.dynamic_slice_in_dim(approx_router, offset, col_width, 1),
    )
    norm_velocity, norm_master = advance(norm_momentum, norm_weight, norm_sum / replicas)
    key_params, router_params, norm_params = (
        lax.all_gather(key_master.astype(jnp.bfloat16), "shard", axis=0, tiled=True),
        lax.all_gather(router_master.astype(jnp.bfloat16), "shard", axis=0, tiled=True),
        lax.all_gather(norm_master.astype(jnp.bfloat16), "shard", axis=1, tiled=True),
    )
    key_carry = (merged_key - approx_key)[None]
    router_carry = (merged_router - approx_router)[None]
    return (
        key_carry,
        router_carry,
        key_velocity,
        key_master,
        key_params,
        router_velocity,
        router_master,
        router_params,
        norm_velocity,
        norm_master,
        norm_params,
    )


def halves(x):
    high = x.astype(bf16)
    return high, (x - high.astype(f32)).astype(bf16)


def fold(x, rows, cols):
    y = x[:rows] + x[rows:]
    return y[:, :cols] + y[:, cols:]


def tile_start(d):
    return (5 * d + 1) // 2


def packed(x):
    pieces = [x[:, LANES * j : LANES * (j + 1)] for j in range(x.shape[1] // LANES)]
    rows = 2 * len(pieces)
    return jnp.concatenate(pieces + [jnp.zeros((16 - rows, LANES), f32)], axis=0)


NT = (((1,), (1,)), ((), ()))


def dot(a, b):
    return jnp.dot(a, b, preferred_element_type=f32)


def dot_nt(a, b):
    return lax.dot_general(a, b, NT, preferred_element_type=f32)


def mul(a, b, product=dot):
    a_high, a_low = halves(a)
    b_high, b_low = halves(b)
    both = product(jnp.concatenate([a_high, a_low], axis=0), b_high)
    rows = a.shape[0]
    return both[:rows] + (both[rows:] + product(a_high, b_low))


def exchange_kernel(
    n_dp, n_shard, rank,
    kg_h, ke_h, rg_h, re_h, kb_h, rb_h, ng_h, nm_h, nw_h, km_h, kw_h, rm_h, rw_h,
    mk, mr, km, kw, rm, rw, nm, nw, lift, cols, ukey, urouter, nsum, npar,
    kg, ke, rg, re, kb, rb, ng,
    mkm, mrm, p64, recv1, recv2, nsend, nrecv, csend, brecv, load, send, recv,
):
    d = lax.axis_index("dp")
    s = lax.axis_index("shard")
    total = n_dp * n_shard
    me = d * n_shard + s
    core = lax.rem(s, 2)
    x = s // 2
    mate = s + 1 - 2 * core
    half = total // 2
    q = x * n_dp + d
    key_rows = mk.shape[0] // 2
    router_rows = mr.shape[0] // 2
    tiles = csend.shape[0] // 2

    pairs = n_dp // 2
    span = mk.shape[1] // pairs
    chunks = [slice(span * p, span * (p + 1)) for p in range(pairs)]
    fetched = {}

    def fetch(name, there, here):
        fetched[name] = pltpu.make_async_copy(there, here, load.at[len(fetched)])
        fetched[name].start()

    def need(*names):
        for name in names:
            fetched[name].wait()

    fetch("rg", rg_h, rg)
    fetch("re", re_h, re)
    fetch("rb", rb_h, rb)
    for p, lanes in enumerate(chunks):
        fetch(("kg", p), kg_h.at[:, :, lanes], kg.at[:, :, lanes])
        fetch(("ke", p), ke_h.at[:, :, lanes], ke.at[:, :, lanes])
        fetch(("kb", p), kb_h.at[:, lanes], kb.at[:, lanes])
    fetch("ng", ng_h, ng)
    fetch("km", km_h, km)
    fetch("kw", kw_h, kw)
    fetch("rm", rm_h, rm)
    fetch("rw", rw_h, rw)
    fetch("nm", nm_h, nm)
    fetch("nw", nw_h, nw)

    def peer_all(j):
        t = lax.rem(me + j, total)
        return (t // n_shard, lax.rem(t, n_shard))

    barrier = pltpu.get_barrier_semaphore()

    def greet(j, carry):
        pl.semaphore_signal(barrier, inc=1, device_id=peer_all(j), device_id_type=MESH)
        return carry

    lax.fori_loop(1, total, greet, 0)

    def put(src, dst, which, device):
        pltpu.make_async_remote_copy(
            src_ref=src, dst_ref=dst, send_sem=send.at[which], recv_sem=recv.at[which],
            device_id=device, device_id_type=MESH,
        ).start()

    def wait_recv(ref, which):
        pltpu.make_async_copy(ref, ref, recv.at[which]).wait()

    def wait_send(ref, which):
        pltpu.make_async_copy(ref, ref, send.at[which]).wait()

    need("rg", "re", "rb")
    high, low = halves(rg[0].astype(f32) + re[0])
    mr[:router_rows] = high
    mr[router_rows:] = low
    mrm[:router_rows] = high
    rb2 = jnp.concatenate(halves(rb[...]), axis=0)
    p64[rank:] = jnp.concatenate(
        [
            fold(dot_nt(rb2, mr[...]), rank, router_rows),
            jnp.zeros((rank, LANES - router_rows), f32),
        ],
        axis=1,
    )
    projected = None
    for p, lanes in enumerate(chunks):
        need(("kg", p), ("ke", p), ("kb", p))
        high, low = halves(kg[0, :, lanes].astype(f32) + ke[0, :, lanes])
        mk[:key_rows, lanes] = high
        mk[key_rows:, lanes] = low
        mkm[:key_rows, lanes] = high
        kb2 = jnp.concatenate(halves(kb[:, lanes]), axis=0)
        term = dot_nt(kb2, jnp.concatenate([high, low], axis=0))
        projected = term if projected is None else projected + term
    p64[:rank] = fold(projected, rank, key_rows)

    pl.semaphore_wait(barrier, total - 1)

    def far_first(count):
        return sorted(range(1, count), key=lambda j: -min(j, count - j))

    for j in far_first(n_dp):
        to = lax.rem(d + j, n_dp)
        put(p64.at[pl.ds(pl.multiple_of(to * 8, 8), 8)], recv1.at[d], 0, (to, s))

    key_half, router_half = pl.ds(key_rows, key_rows), pl.ds(router_rows, router_rows)

    @pl.when(core == 1)
    def _():
        put(mk.at[pl.ds(0, key_rows)], mkm.at[key_half], 5, (d, mate))

    @pl.when(core == 0)
    def _():
        put(mr.at[pl.ds(0, router_rows)], mrm.at[router_half], 5, (d, mate))

    recv1[d] = p64[pl.ds(pl.multiple_of(d * 8, 8), 8), :]
    need("ng")
    nsend[0] = packed(ng[0].astype(f32)).astype(bf16)
    nrecv[d] = nsend[0]
    need("km", "kw", "rm", "rw")
    decay = learning_rate * momentum_decay
    ukey[s] = (kw[...] - decay * km[...]).astype(bf16)
    urouter[s] = (rw[...] - decay * rm[...]).astype(bf16)
    wait_recv(recv1.at[pl.ds(0, n_dp - 1)], 0)
    slot = s * n_dp + d
    recv2[slot] = jnp.sum(recv1[...], axis=0)
    summed = recv2.at[slot]
    for j in far_first(n_dp):
        put(summed, summed, 2, (lax.rem(d + j, n_dp), s))
    for j in far_first(n_dp) + [0]:
        put(summed, summed, 2, (lax.rem(d + j, n_dp), mate))
    for j in far_first(n_dp) + [0]:
        for other in range(2):
            put(summed, summed, 12, (lax.rem(d + j, n_dp), 2 * (1 - x) + other))

    wait_recv(recv2.at[pl.ds(0, half - 1)], 2)

    def factor(which, first):
        count = rank // 8
        return recv2[pl.ds(which * n_dp + first * count, count)].reshape(rank, LANES)

    def stacked(own, other):
        return jnp.concatenate(halves(jnp.concatenate([own, other], axis=1)), axis=0)

    per_pair = tiles // pairs

    def columns_of(owner, left, merged):
        for step in (2, 1, 3, 0):
            p = lax.rem(d // 2 + step, pairs)
            lanes = pl.ds(pl.multiple_of(p * span, LANES), span)
            out = dot(left, merged[:, lanes])
            part = (out[:rank] + out[rank:]).astype(bf16)
            for k in range(2):
                for j in range(per_pair):
                    csend[k * tiles + per_pair * p + j] = part[
                        16 * k : 16 * k + 16, LANES * j : LANES * (j + 1)
                    ]
            for k in range(2):
                for odd, first, count in ((0, 0, 3), (1, 3, 2)):
                    to_d = 2 * p + odd

                    def send_part():
                        put(
                            csend.at[pl.ds(k * tiles + per_pair * p + first, count)],
                            brecv.at[q, pl.ds(0, count)], 6, (to_d, 2 * k + owner),
                        )

                    if step:
                        send_part()
                    else:
                        pl.when(jnp.logical_or(x != k, to_d != d))(send_part)

    @pl.when(core == 0)
    def _():
        left = stacked(factor(s, 0), factor(mate, 0))
        wait_recv(mkm.at[key_half], 5)
        columns_of(0, left, mkm)

    @pl.when(core == 1)
    def _():
        left = stacked(factor(s, 1)[:, :router_rows], factor(mate, 1)[:, :router_rows])
        wait_recv(mrm.at[router_half], 5)
        columns_of(1, left, mrm)

    for j in range(1, n_dp):
        put(nsend.at[0], nrecv.at[d], 1, (lax.rem(d + j, n_dp), s))

    for j in range(1, n_shard):
        to = (d, lax.rem(s + j, n_shard))
        put(ukey.at[s], ukey.at[s], 3, to)
        put(urouter.at[s], urouter.at[s], 9, to)

    wait_recv(recv2.at[pl.ds(0, half)], 12)

    both = 2 * rank
    rows = jnp.concatenate(
        [recv2[n_dp * k : n_dp * (k + 1)].reshape(both, LANES) for k in range(n_shard)], axis=1
    )
    down = lax.broadcasted_iota(jnp.int32, (both, both), 0)
    along = lax.broadcasted_iota(jnp.int32, (both, both), 1)
    gram = jnp.where((down < rank) == (along < rank), mul(rows, rows, dot_nt), 0.0)
    identity = jnp.where(down == along, 1.0, 0.0).astype(f32)
    square = gram * gram
    scale_key = jnp.sqrt(jnp.sum(square[:rank], keepdims=True)) + 1e-06
    scale_router = jnp.sqrt(jnp.sum(square[rank:], keepdims=True)) + 1e-06
    row_index = lax.broadcasted_iota(jnp.int32, (both, 1), 0)
    scaling = jnp.where(row_index < rank, scale_key, scale_router)
    t = gram / scaling
    middle = 1.5 * identity - 0.5 * t
    root = middle
    for step in range(1, ROOT_STEPS):
        t = mul(t, 2.25 * identity - 1.5 * t + 0.25 * mul(t, t))
        middle = 1.5 * identity - 0.5 * t
        if step < ROOT_STEPS - 1:
            root = mul(middle, root)
    root = mul(middle, root)
    lift[...] = mul(root, mul(root, rows)) / scaling

    need("nm", "nw")
    wait_recv(nrecv.at[pl.ds(0, n_dp - 1)], 1)
    norm_sum = jnp.sum(nrecv[...].astype(f32), axis=0)
    nsum[...] = norm_sum
    norm_velocity, norm_master = advance(packed(nm[...]), packed(nw[...]), norm_sum / n_dp)
    npar[s] = norm_master.astype(bf16)
    for j in range(1, n_shard):
        put(npar.at[s], npar.at[s], 4, (d, lax.rem(s + j, n_shard)))

    def peer_core(j):
        to = lax.rem(q + j, half)
        return to // n_dp, lax.rem(to, n_dp)

    offset = x * tiles + tile_start(d)
    mine = core * 2 * tiles + offset
    for parity, count in ((0, 3), (1, 2)):

        @pl.when(lax.rem(d, 2) == parity)
        def _():
            brecv[q, :count] = csend[pl.ds(offset, count)]
            wait_recv(cols.at[pl.ds(0, (half - 1) * count)], 6)
            added = jnp.sum(brecv[:, :count].astype(f32), axis=0) / n_dp
            cols[pl.ds(mine, count)] = added.astype(bf16)

            there = cols.at[pl.ds(mine, count)]
            for j in far_first(half):
                to_x, to_d = peer_core(j)
                put(there, there, 7 + 3 * lax.rem(to_x + x, 2), (to_d, to_x * 2 + core))
            wait_recv(cols.at[pl.ds(0, tiles - count)], 7)

    ours = cols.at[pl.ds(core * 2 * tiles + x * tiles, tiles)]
    put(ours, ours, 8, (d, mate))
    theirs = cols.at[pl.ds(core * 2 * tiles + (1 - x) * tiles, tiles)]
    wait_recv(theirs, 10)
    put(theirs, theirs, 11, (d, mate))

    wait_recv(ukey.at[pl.ds(0, n_shard - 1)], 3)
    wait_recv(urouter.at[pl.ds(0, n_shard - 1)], 9)
    wait_recv(npar.at[pl.ds(0, n_shard - 1)], 4)
    wait_send(recv1.at[pl.ds(0, n_dp - 1)], 0)
    wait_send(nrecv.at[pl.ds(0, n_dp - 1)], 1)
    wait_send(recv2.at[pl.ds(0, half - 1)], 2)
    wait_send(recv2.at[pl.ds(0, half)], 12)
    wait_send(ukey.at[pl.ds(0, n_shard - 1)], 3)
    wait_send(urouter.at[pl.ds(0, n_shard - 1)], 9)
    wait_send(npar.at[pl.ds(0, n_shard - 1)], 4)

    @pl.when(core == 1)
    def _():
        wait_send(mkm.at[key_half], 5)

    @pl.when(core == 0)
    def _():
        wait_send(mrm.at[router_half], 5)

    for parity, count in ((0, 3), (1, 2)):

        @pl.when(lax.rem(d, 2) == parity)
        def _():
            wait_send(csend.at[pl.ds(0, 2 * tiles - count)], 6)
            wait_send(cols.at[pl.ds(0, (n_dp - 1) * count)], 7)
            wait_send(cols.at[pl.ds(0, n_dp * count)], 10)

    wait_send(ours, 8)
    wait_send(theirs, 11)
    wait_recv(ours, 8)
    wait_recv(theirs, 11)


def finish_kernel(
    n_dp, n_shard, rank,
    mk, mr, km, kw, rm, rw, nm, nw, lift, cols, ukey, urouter, nsum, npar,
    key_carry, router_carry, key_velocity, key_master, key_params,
    router_velocity, router_master, router_params, norm_velocity, norm_master, norm_params,
    ck, cr,
):
    d = lax.axis_index("dp")
    s = lax.axis_index("shard")
    key_rows, router_rows = mk.shape[0] // 2, mr.shape[0] // 2
    span = km.shape[0]
    tiles = cols.shape[0] // 4
    for core, where in ((0, ck), (1, cr)):
        for k in range(2):
            for j in range(tiles):
                piece = cols[(core * 2 + k) * tiles + j]
                lanes = slice(LANES * j, LANES * (j + 1))
                where[16 * k : 16 * k + 16, lanes] = piece
                where[rank + 16 * k : rank + 16 * k + 16, lanes] = piece

    def turned(factor):
        return jnp.concatenate(halves(factor.T), axis=1)

    own = lift[:, pl.ds(pl.multiple_of(s * LANES, LANES), LANES)]
    own_key = turned(own[:rank])
    own_router = turned(own[rank:])[:router_rows]
    merged = mk[:key_rows].astype(f32) + mk[key_rows:].astype(f32)
    key_carry[0] = merged - dot(own_key, ck[...])
    merged = mr[:router_rows].astype(f32) + mr[router_rows:].astype(f32)
    router_carry[0] = merged - dot(own_router, cr[...])

    def block(core):
        parts = []
        for k in range(2):
            near = cols[pl.ds((core * 2 + k) * tiles + 5 * d // 2, 3)].astype(f32)
            parts.append(jnp.concatenate([near[0], near[1], near[2]], axis=1))
        both = jnp.concatenate(parts, axis=0)
        extra = both.shape[1] - span
        return jnp.where(lax.rem(d, 2) == 1, both[:, extra:], both[:, :span])

    turned_block = block(0).T.astype(bf16)
    key_block = jnp.concatenate([turned_block, turned_block], axis=1)
    router_block = block(1).astype(bf16)
    router_block = jnp.concatenate([router_block, router_block], axis=0)
    key_velocity[...], key_master[...] = advance(
        km[...], kw[...], dot(key_block, jnp.concatenate(halves(own[:rank]), axis=0))
    )
    router_velocity[...], router_master[...] = advance(
        rm[...], rw[...], dot(own_router, router_block)
    )
    approx = dot(key_block, jnp.concatenate(halves(lift[:rank]), axis=0))
    for k in range(n_shard):
        lanes = slice(key_rows * k, key_rows * (k + 1))
        key_params[:, lanes] = (
            ukey[k].astype(f32) - learning_rate * approx[:, lanes]
        ).astype(bf16)
        factor = turned(lift[rank:, LANES * k : LANES * (k + 1)])[:router_rows]
        router_params[router_rows * k : router_rows * (k + 1)] = (
            urouter[k].astype(f32) - learning_rate * dot(factor, router_block)
        ).astype(bf16)

    pieces = nm.shape[1] // LANES

    def unpacked(x):
        return jnp.concatenate([x[2 * j : 2 * j + 2] for j in range(pieces)], axis=1)

    norm_velocity[...], norm_master[...] = advance(nm[...], nw[...], unpacked(nsum[...]) / n_dp)
    norm_params[...] = jnp.concatenate(
        [unpacked(npar[k].astype(f32)) for k in range(n_shard)], axis=1
    ).astype(bf16)


def fast_body(
    n_dp, n_shard,
    key_grad, key_error, router_grad, router_error, norm_grad, key_basis, router_basis,
    key_momentum, key_weight, router_momentum, router_weight, norm_momentum, norm_weight,
):
    rank, width = key_basis.shape
    key_rows, router_rows = key_grad.shape[1], router_grad.shape[1]
    span = key_momentum.shape[1]
    total, half, tiles = n_dp * n_shard, n_dp * n_shard // 2, width // LANES
    vmem = pl.BlockSpec(memory_space=pltpu.VMEM)
    hbm = pl.BlockSpec(memory_space=pltpu.HBM)
    shape = jax.ShapeDtypeStruct
    key_state, router_state = shape((span, key_rows), f32), shape((router_rows, span), f32)
    norm_state = shape(norm_momentum.shape, f32)
    middle = pl.pallas_call(
        functools.partial(exchange_kernel, n_dp, n_shard, rank),
        out_shape=[
            shape((2 * key_rows, width), bf16),
            shape((2 * router_rows, width), bf16),
            key_state,
            key_state,
            router_state,
            router_state,
            norm_state,
            norm_state,
            shape((2 * rank, n_shard * LANES), f32),
            shape((4 * tiles, 16, LANES), bf16),
            shape((n_shard, span, key_rows), bf16),
            shape((n_shard, router_rows, span), bf16),
            shape((16, LANES), f32),
            shape((n_shard, 16, LANES), bf16),
        ],
        in_specs=[hbm] * 13,
        out_specs=[vmem] * 14,
        scratch_shapes=[
            pltpu.VMEM(key_grad.shape, bf16),
            pltpu.VMEM(key_error.shape, f32),
            pltpu.VMEM(router_grad.shape, bf16),
            pltpu.VMEM(router_error.shape, f32),
            pltpu.VMEM(key_basis.shape, f32),
            pltpu.VMEM(router_basis.shape, f32),
            pltpu.VMEM(norm_grad.shape, bf16),
            pltpu.VMEM((2 * key_rows, width), bf16),
            pltpu.VMEM((2 * router_rows, width), bf16),
            pltpu.VMEM((2 * rank, LANES), f32),
            pltpu.VMEM((n_dp, 8, LANES), f32),
            pltpu.VMEM((total, 8, LANES), f32),
            pltpu.VMEM((1, 16, LANES), bf16),
            pltpu.VMEM((n_dp, 16, LANES), bf16),
            pltpu.VMEM((2 * tiles, 16, LANES), bf16),
            pltpu.VMEM((half, 3, 16, LANES), bf16),
            pltpu.SemaphoreType.DMA((10 + 3 * n_dp // 2,)),
            pltpu.SemaphoreType.DMA((13,)),
            pltpu.SemaphoreType.DMA((13,)),
        ],
        compiler_params=pltpu.CompilerParams(
            collective_id=0, has_side_effects=True, vmem_limit_bytes=24 * 2**20
        ),
        name="exchange",
    )(
        *(
            pltpu.with_memory_space_constraint(operand, pltpu.HBM)
            for operand in (
                key_grad, key_error, router_grad, router_error, key_basis, router_basis, norm_grad,
                norm_momentum, norm_weight, key_momentum.T, key_weight.T, router_momentum,
                router_weight,
            )
        )
    )
    results = pl.pallas_call(
        functools.partial(finish_kernel, n_dp, n_shard, rank),
        out_shape=[
            shape(key_error.shape, f32),
            shape(router_error.shape, f32),
            key_state,
            key_state,
            shape((span, n_shard * key_rows), bf16),
            router_state,
            router_state,
            shape((n_shard * router_rows, span), bf16),
            norm_state,
            norm_state,
            shape((norm_momentum.shape[0], width), bf16),
        ],
        in_specs=[vmem] * 14,
        out_specs=[vmem] * 11,
        scratch_shapes=[
            pltpu.VMEM((2 * rank, width), bf16),
            pltpu.VMEM((2 * rank, width), bf16),
        ],
        compiler_params=pltpu.CompilerParams(vmem_limit_bytes=24 * 2**20),
        name="finish",
    )(*middle)
    return tuple(y.T if i in (2, 3, 4) else y for i, y in enumerate(results))


def solution(mesh):
    n_dp, n_shard = mesh.shape["dp"], mesh.shape["shard"]

    def body(*arrays):
        key_grad, router_grad, key_basis = arrays[0], arrays[2], arrays[5]
        rank, width = key_basis.shape
        tiled = (
            2 * rank == 8 * n_dp == 16 * n_shard
            and key_grad.shape[1] == LANES
            and router_grad.shape[1] == 16
            and 2 * width == 5 * LANES * n_dp
            and arrays[11].shape == (2, 5 * LANES)
        )
        if tiled:
            return fast_body(n_dp, n_shard, *arrays)
        return general_body(*arrays)

    return jax.shard_map(
        body,
        mesh=mesh,
        in_specs=(
            P("dp", "shard", None),
            P("dp", "shard", None),
            P("dp", "shard", None),
            P("dp", "shard", None),
            P("dp", None, "shard"),
            P(),
            P(),
            P("shard", "dp"),
            P("shard", "dp"),
            P("shard", "dp"),
            P("shard", "dp"),
            P(None, "shard"),
            P(None, "shard"),
        ),
        out_specs=(
            P("dp", "shard", None),
            P("dp", "shard", None),
            P("shard", "dp"),
            P("shard", "dp"),
            P(None, "dp"),
            P("shard", "dp"),
            P("shard", "dp"),
            P(None, "dp"),
            P(None, "shard"),
            P(None, "shard"),
            P(),
        ),
        check_vma=False,
    )
```
